256 devices in a mesh: section: 16 (over x_hi, y, core), expert: 16 (over z, x_lo).
Axes of the slice: x: 4 (x_hi: 2, x_lo: 2; x = x_hi * 2 + x_lo), y: 4, z: 8, core: 2. Of those that a mesh axis runs over, the one named last changes fastest.
Arguments:
- forward_in: bfloat16 [16, 2048, 7168], P('section', 'expert'), may hold values from -6 to 6
- backward_saved: bfloat16 [16, 2048, 7168], P('section', 'expert'), may hold values from -6 to 6
- backward_grad: bfloat16 [16, 2048, 7168], P('section', 'expert'), may hold values from -6 to 6
- forward_routes: int32 [16, 2048, 2], P('section', 'expert'), may hold values from 0 to 127, as said below
- forward_gates: float32 [16, 2048, 2], P('section', 'expert'), may hold values from 0.2 to 1
- backward_routes: int32 [16, 2048, 2], P('section', 'expert'), may hold values from 0 to 127, as said below
- backward_gates: float32 [16, 2048, 2], P('section', 'expert'), may hold values from 0.2 to 1
- up_weight: bfloat16 [16, 7168, 2432], P('section', 'expert'), may hold values from -0.0625 to 0.0625
- down_weight: bfloat16 [16, 2432, 7168], P('section', None, 'expert'), may hold values from -0.125 to 0.125
Outputs:
- forward_out: bfloat16 [16, 2048, 7168], P('section', 'expert')
- backward_out: bfloat16 [16, 2048, 7168], P('section', 'expert')
The draws below stay inside these ranges and needn't reach their ends.
Inputs may be any that keep to these rules, and one draw needn't show every extreme that they name: `forward_routes`: in every row the two ids differ. Of the 128 rows of one device (aligned blocks of a section), at most 17 name expert 0, and on some device exactly 17 do. `backward_routes`: in every row the two ids differ. Of the 128 rows of one device (aligned blocks of a section), at most 17 name expert 0, and on some device exactly 17 do.
All inputs are finite; a program needn't handle non-finite values.
Results may differ from the reference program's by a relative error of at most 0.005.
Values may be sent and summed in bfloat16 or wider, within the bound.
No kernel may reach another device: no remote copies, remote signals or barrier semaphores. Data moves between devices by JAX's collectives and lax.ppermute only.
A program may use at most 128 MiB of HBM per device.

```python
import jax
import jax.numpy as jnp
from jax import lax

D = 7168
EXPERTS = 128
FF = 2432
TOK_DEV = 128
MOST = 17
TOKENS = 2048
N_SECTION = 16
N_EXPERT = 16


def route_table(key):
    blocks = N_SECTION * N_EXPERT
    keys = jax.random.split(key, 6)
    counts = jax.random.randint(keys[0], (blocks,), MOST // 2, MOST + 1)
    top_block = jax.random.randint(keys[1], (), 0, blocks)
    counts = jnp.where(jnp.arange(blocks) == top_block, MOST, counts)
    ranking = jax.vmap(lambda single: jax.random.permutation(single, TOK_DEV))(jax.random.split(keys[2], blocks))
    chosen = ranking < counts[:, None]
    placing = jax.random.randint(keys[3], (blocks, TOK_DEV), 0, 2)
    first_id = jax.random.randint(keys[4], (blocks, TOK_DEV), 1, EXPERTS)
    offset = jax.random.randint(keys[5], (blocks, TOK_DEV), 1, EXPERTS - 1)
    second_id = 1 + (first_id - 1 + offset) % (EXPERTS - 1)
    second_id = jnp.where(chosen, 0, second_id)
    left_id = jnp.where(placing == 0, first_id, second_id)
    right_id = jnp.where(placing == 0, second_id, first_id)
    paired = jnp.stack([left_id, right_id], axis=-1)
    return paired.reshape(N_SECTION, N_EXPERT * TOK_DEV, 2).astype(jnp.int32)


def draw_forward_routes(key, part):
    key = jax.random.fold_in(key, 3)
    return route_table(key)


def draw_backward_routes(key, part):
    key = jax.random.fold_in(key, 5)
    return route_table(key)


def steps_of(rng, extent, cuts, smallest, top_value):
    level = 1.0
    for position, blocks in cuts:
        draws = jax.random.uniform(jax.random.fold_in(jax.random.fold_in(rng, 6), position), (blocks,), jnp.float32, smallest / len(cuts), top_value / len(cuts))
        level = level * jnp.repeat(jnp.exp(draws), extent[position] // blocks).reshape((-1,) + (1,) * (len(extent) - 1 - position))
    return level


def noise(stream_key, dims, spread, most, cuts=(), held_as=jnp.bfloat16):
    values = jax.random.normal(stream_key, dims, jnp.float32) * spread
    if len(cuts) > 0:
        values = steps_of(stream_key, dims, cuts, -0.22, 0.18) * values
    return jnp.clip(values, min=-most, max=most).astype(held_as)


def setup_inputs(seed: int = 0) -> dict:
    key_of = jax.random.split(jax.random.key(seed), 10)
    forward_in = noise(key_of[0], (N_SECTION, TOKENS, D), 1.0, 6.0, ((0, 16), (1, 16)))
    backward_saved = noise(key_of[1], (N_SECTION, TOKENS, D), 1.0, 6.0, ((0, 16), (1, 16)))
    backward_grad = noise(key_of[2], (N_SECTION, TOKENS, D), 1.0, 6.0, ((0, 16), (1, 16)))
    forward_routes = draw_forward_routes(jax.random.fold_in(key_of[9], 71), 0)
    forward_gates = jnp.clip(0.2 + 0.8 * jax.random.uniform(key_of[4], (N_SECTION, TOKENS, 2), jnp.float32) ** steps_of(key_of[4], (N_SECTION, TOKENS, 2), ((0, 16), (1, 16)), -0.2, 0.2), 0.2, 1.0)
    backward_routes = draw_backward_routes(jax.random.fold_in(key_of[9], 71), 0)
    backward_gates = jnp.clip(0.2 + 0.8 * jax.random.uniform(key_of[6], (N_SECTION, TOKENS, 2), jnp.float32) ** steps_of(key_of[6], (N_SECTION, TOKENS, 2), ((0, 16), (1, 16)), -0.2, 0.2), 0.2, 1.0)
    up_weight = noise(key_of[7], (N_SECTION, D, FF), D ** -0.5, 0.0625, ((0, 16), (1, 16)))
    down_weight = noise(key_of[8], (N_SECTION, FF, D), FF ** -0.5, 0.125, ((0, 16), (2, 16)))
    return dict(forward_in=forward_in, backward_saved=backward_saved, backward_grad=backward_grad, forward_routes=forward_routes, forward_gates=forward_gates, backward_routes=backward_routes, backward_gates=backward_gates, up_weight=up_weight, down_weight=down_weight)


def window_pack(routes, gate_vals, capacity):
    hitting = routes == 0
    scaling = jnp.sum(jnp.where(hitting, gate_vals, jnp.zeros_like(gate_vals)), axis=1)
    routed = jnp.any(hitting, axis=1)
    slot_rows = jnp.nonzero(routed, size=capacity, fill_value=0)[0].astype(jnp.int32)
    live_count = jnp.sum(routed.astype(jnp.int32))
    slot_live = (jnp.arange(capacity, dtype=jnp.int32) < live_count).astype(jnp.float32)
    slot_gate = scaling[slot_rows] * slot_live
    return slot_rows, slot_gate, slot_live


def silu_slope(before):
    sigma = jax.nn.sigmoid(before)
    return sigma * (1.0 + before * (1.0 - sigma))


def layer_forward(acts, routes, gate_vals, up_local, down_local):
    slot_rows, slot_gate, slot_live = window_pack(routes, gate_vals, N_EXPERT * MOST)
    picked = acts[slot_rows]
    before = jnp.dot(picked, up_local, preferred_element_type=jnp.float32)
    hidden = jax.nn.silu(before).astype(jnp.bfloat16)
    branch = jnp.dot(hidden, down_local, preferred_element_type=jnp.float32).astype(jnp.bfloat16)
    branch = lax.optimization_barrier(branch)
    summed = acts.astype(jnp.float32).at[slot_rows].add(slot_gate[:, None] * branch.astype(jnp.float32))
    return summed.astype(jnp.bfloat16)


def layer_backward(saved, cotangent, routes, gate_vals, up_local, down_local):
    slot_rows, slot_gate, slot_live = window_pack(routes, gate_vals, N_EXPERT * MOST)
    picked = saved[slot_rows]
    upstream = (slot_gate[:, None] * cotangent[slot_rows].astype(jnp.float32)).astype(jnp.bfloat16)
    before = jnp.dot(picked, up_local, preferred_element_type=jnp.float32)
    hidden_grad = lax.dot_general(upstream, down_local, (((1,), (1,)), ((), ())), preferred_element_type=jnp.float32)
    pre_grad = (hidden_grad * silu_slope(before)).astype(jnp.bfloat16)
    back = lax.dot_general(pre_grad, up_local, (((1,), (1,)), ((), ())), preferred_element_type=jnp.float32).astype(jnp.bfloat16)
    back = lax.optimization_barrier(back)
    summed = cotangent.astype(jnp.float32).at[slot_rows].add(slot_live[:, None] * back.astype(jnp.float32))
    return summed.astype(jnp.bfloat16)


def forward_item(items):
    return layer_forward(items[0], items[1], items[2], items[3], items[4])


def backward_item(items):
    return layer_backward(items[0], items[1], items[2], items[3], items[4], items[5])


def reference(forward_in, backward_saved, backward_grad, forward_routes, forward_gates, backward_routes, backward_gates, up_weight, down_weight):
    forward_done = lax.map(forward_item, (forward_in, forward_routes, forward_gates, up_weight, down_weight))
    backward_done = lax.map(backward_item, (backward_saved, backward_grad, backward_routes, backward_gates, up_weight, down_weight))
    return jnp.roll(forward_done, 1, axis=0), jnp.roll(backward_done, -1, axis=0)
```

```python
import functools

import jax
import jax.numpy as jnp
from jax import lax
from jax.experimental import pallas as pl
from jax.experimental.pallas import tpu as pltpu
from jax.sharding import PartitionSpec as P

MOST = 17
TOK = 128
D = 7168
FF = 2432
COLS = 448
NODES = 8
PICK = 56
CHUNK = 104
SENT = 72
BACK = 40
ROWS = 24
FIRST = 1280
BF = jnp.bfloat16
F32 = jnp.float32
VMEM_LIMIT = 48 * 1024 * 1024


def iota(shape, dim):
    return lax.broadcasted_iota(jnp.int32, shape, dim)


def dot(left, right):
    return jnp.dot(left, right, preferred_element_type=F32)


def dot_tn(left, right):
    return lax.dot_general(left, right, (((0,), (0,)), ((), ())), preferred_element_type=F32)


def dot_nt(left, right):
    return lax.dot_general(left, right, (((1,), (1,)), ((), ())), preferred_element_type=F32)


def onehot(cond):
    return jnp.where(cond, 1.0, 0.0).astype(BF)


def token_columns(routes, gates):
    hits = routes == 0
    hit = jnp.sum(jnp.where(hits, 1.0, 0.0), axis=1, keepdims=True)
    scaling = jnp.sum(jnp.where(hits, gates, 0.0), axis=1, keepdims=True)
    return hit, scaling


def across(column):
    wide = jnp.broadcast_to(column, (TOK, TOK)).astype(BF)
    eye = onehot(iota((TOK, TOK), 0) == iota((TOK, TOK), 1))
    return dot_tn(wide, eye)


def slot_rows(hit):
    wide = jnp.broadcast_to(hit, (TOK, TOK)).astype(BF)
    upto = onehot(iota((TOK, TOK), 0) <= iota((TOK, TOK), 1))
    rank = dot_tn(wide, upto)
    return jnp.where(across(hit) > 0.5, rank - 1.0, -1.0)


def placed(slots, rows, start):
    row = iota((rows, TOK), 0) - start
    return (slots[:rows] == row.astype(F32)) & (row >= 0)


def pick_kernel(froutes, fgates, broutes, bgates, acts, saved, cot, packed, kept, gate, meta, px, ps, pu, scale):
    @pl.when(pl.program_id(0) == 0)
    def _():
        fhit, fscaling = token_columns(froutes[...], fgates[...])
        bhit, bscaling = token_columns(broutes[...], bgates[...])
        fslots = slot_rows(fhit)
        bslots = slot_rows(bhit)
        px[...] = onehot(placed(fslots, PICK, 0))
        ps[...] = onehot(placed(bslots, PICK, MOST))
        pu[...] = onehot(placed(bslots, PICK, 2 * MOST))
        scale[...] = jnp.broadcast_to(bscaling, (TOK, TOK))
        hi = fscaling.astype(BF).astype(F32)
        mid = (fscaling - hi).astype(BF).astype(F32)
        low = fscaling - hi - mid
        frow = across(hi) + across(mid) + across(low)
        mine = jnp.sum(jnp.where(placed(fslots, ROWS, 0), frow[:ROWS], 0.0), axis=1, keepdims=True)
        gate[...] = jnp.broadcast_to(mine, (ROWS, TOK))
        meta[0] = fslots[:ROWS]
        meta[1] = bslots[:ROWS]

    x = acts[...]
    raw = cot[...]
    wide = jnp.concatenate([scale[...]] * 7, axis=1)
    upstream = (wide * raw.astype(F32)).astype(BF)
    fpart = dot(px[...], x)
    rows = fpart + dot(ps[...], saved[...]) + dot(pu[...], upstream)
    rows = rows.astype(BF)
    packed[0] = rows[:, :COLS]
    packed[1] = rows[:, COLS:]
    kept[0] = fpart.astype(BF)[:ROWS]
    here = iota((ROWS, PICK), 0)
    down = onehot((iota((ROWS, PICK), 1) == here + 2 * MOST) & (here < MOST))
    kept[1] = dot(down, dot(pu[...], raw).astype(BF)).astype(BF)


def pick(froutes, fgates, broutes, bgates, acts, saved, cot):
    width = 2 * COLS
    whole = lambda i: (0, 0)
    small = pl.BlockSpec((TOK, 2), whole)
    strip = pl.BlockSpec((TOK, width), lambda i: (0, i))
    return pl.pallas_call(
        pick_kernel,
        grid=(NODES,),
        out_shape=(
            jax.ShapeDtypeStruct((2 * NODES, PICK, COLS), BF),
            jax.ShapeDtypeStruct((2, ROWS, D), BF),
            jax.ShapeDtypeStruct((ROWS, TOK), F32),
            jax.ShapeDtypeStruct((2, ROWS, TOK), F32),
        ),
        in_specs=[small, small, small, small, strip, strip, strip],
        out_specs=(
            pl.BlockSpec((2, PICK, COLS), lambda i: (i, 0, 0)),
            pl.BlockSpec((2, ROWS, width), lambda i: (0, 0, i)),
            pl.BlockSpec((ROWS, TOK), whole),
            pl.BlockSpec((2, ROWS, TOK), lambda i: (0, 0, 0)),
        ),
        scratch_shapes=[
            pltpu.VMEM((PICK, TOK), BF),
            pltpu.VMEM((PICK, TOK), BF),
            pltpu.VMEM((PICK, TOK), BF),
            pltpu.VMEM((TOK, TOK), F32),
        ],
        compiler_params=pltpu.CompilerParams(vmem_limit_bytes=VMEM_LIMIT),
        name="pick",
    )(froutes, fgates, broutes, bgates, acts, saved, cot)


def spread(owner):
    r, c = iota((CHUNK, PICK), 0), iota((CHUNK, PICK), 1)
    out = None
    for start, source in ((0, MOST), (2 * MOST, 2 * MOST), (4 * MOST, 0)):
        j = r - start - owner * MOST
        here = (j >= 0) & (j < MOST) & (c == j + source)
        out = here if out is None else out | here
    return onehot(out)


def partial_kernel(node, picks, up, down, out, big):
    @pl.when(pl.program_id(0) == 0)
    def _():
        e0, e1 = spread(0), spread(1)
        for k in range(NODES):
            at = 2 * lax.rem(node[0] + k, NODES)
            both = dot(e0, picks[at]) + dot(e1, picks[at + 1])
            big[pl.ds(k * CHUNK, CHUNK), :] = both.astype(BF)

    rows = big[...]
    ups = dot(rows, up[...]).astype(BF)
    downs = dot_nt(rows, down[...]).astype(BF)
    for k in range(NODES):
        r = iota((CHUNK, ups.shape[1]), 0)
        mine = slice(k * CHUNK, (k + 1) * CHUNK)
        out[k] = jnp.where((r >= 2 * MOST) & (r < 4 * MOST), downs[mine], ups[mine])


def partial_sums(node, picks, up, down):
    width = 256
    return pl.pallas_call(
        partial_kernel,
        grid=(pl.cdiv(FF, width),),
        out_shape=jax.ShapeDtypeStruct((NODES, CHUNK, FF), BF),
        in_specs=[
            pl.BlockSpec(memory_space=pltpu.SMEM),
            pl.BlockSpec((2 * NODES, PICK, COLS), lambda i: (0, 0, 0)),
            pl.BlockSpec((COLS, width), lambda i: (0, i)),
            pl.BlockSpec((width, COLS), lambda i: (i, 0)),
        ],
        out_specs=pl.BlockSpec((NODES, CHUNK, width), lambda i: (0, 0, i)),
        scratch_shapes=[pltpu.VMEM((NODES * CHUNK, COLS), BF)],
        compiler_params=pltpu.CompilerParams(vmem_limit_bytes=VMEM_LIMIT),
        name="partials",
    )(node, picks, up, down)


def gather_rows(owner, start):
    r, c = iota((BACK, SENT), 0), iota((BACK, SENT), 1)
    j = r - start
    return onehot((j >= 0) & (j < MOST) & (c == j + 2 * start + owner * MOST))


def outward_kernel(node, up, down, *refs):
    *parts, out, first, second = refs
    space = 80
    for k in range(NODES):
        if k == 4:
            pieces = parts[8:12]
            for held, head, tail in ((first, pieces[0], pieces[1]), (second, pieces[2], pieces[3])):
                held[pl.ds(k * space, 32), :] = head[...]
                held[pl.ds(k * space + 32, SENT - 32), :] = tail[...]
        else:
            at = 2 * k if k < 4 else 2 * k + 2
            first[pl.ds(k * space, SENT), :] = parts[at][...]
            second[pl.ds(k * space, SENT), :] = parts[at + 1][...]
    branch = (dot(first[...], down[:FIRST, :]) + dot(second[...], down[FIRST:, :])).astype(BF)
    back = (dot_nt(first[...], up[:, :FIRST]) + dot_nt(second[...], up[:, FIRST:])).astype(BF)
    for k in range(NODES):
        mine = slice(k * space, k * space + SENT)
        at = 2 * lax.rem(node[0] + NODES - k, NODES)
        for owner in range(2):
            rows = dot(gather_rows(owner, 0), branch[mine]) + dot(gather_rows(owner, MOST), back[mine])
            out[at + owner] = rows.astype(BF)


def outward(node, up, down, parts):
    vmem = pl.BlockSpec(memory_space=pltpu.VMEM)
    return pl.pallas_call(
        outward_kernel,
        out_shape=jax.ShapeDtypeStruct((2 * NODES, BACK, COLS), BF),
        in_specs=[pl.BlockSpec(memory_space=pltpu.SMEM)] + [vmem] * (2 + len(parts)),
        out_specs=vmem,
        scratch_shapes=[pltpu.VMEM((NODES * 80, FIRST), BF), pltpu.VMEM((NODES * 80, FF - FIRST), BF)],
        compiler_params=pltpu.CompilerParams(vmem_limit_bytes=VMEM_LIMIT),
        name="outward",
    )(node, up, down, *parts)


def row_kernel(back, kept, gate, meta, fout, bout):
    both = jnp.concatenate([back[0], back[1]], axis=1)
    r, c = iota((ROWS, BACK), 0), iota((ROWS, BACK), 1)
    branch = dot(onehot((r < MOST) & (c == r)), both)
    grads = dot(onehot((r < MOST) & (c == r + MOST)), both)
    wide = jnp.concatenate([gate[...]] * 7, axis=1)
    fmeta = jnp.concatenate([meta[0]] * 7, axis=1)
    bmeta = jnp.concatenate([meta[1]] * 7, axis=1)
    live = iota(wide.shape, 0) < MOST
    fout[...] = jnp.where(live, kept[0].astype(F32) + wide * branch, fmeta).astype(BF)
    bout[...] = jnp.where(live, kept[1].astype(F32) + grads, bmeta).astype(BF)


def new_rows(back, kept, gate, meta):
    width = 2 * COLS
    return pl.pallas_call(
        row_kernel,
        grid=(NODES,),
        out_shape=(jax.ShapeDtypeStruct((ROWS, D), BF),) * 2,
        in_specs=[
            pl.BlockSpec((2, BACK, COLS), lambda i: (i, 0, 0)),
            pl.BlockSpec((2, ROWS, width), lambda i: (0, 0, i)),
            pl.BlockSpec((ROWS, TOK), lambda i: (0, 0)),
            pl.BlockSpec((2, ROWS, TOK), lambda i: (0, 0, 0)),
        ],
        out_specs=(pl.BlockSpec((ROWS, width), lambda i: (0, i)),) * 2,
        compiler_params=pltpu.CompilerParams(vmem_limit_bytes=VMEM_LIMIT),
        name="new_rows",
    )(back, kept, gate, meta)


def patch_kernel(fraw, frows, fhead, braw, brows, bhead, fout, bout):
    for raw, rows, head, out in ((fraw, frows, fhead, fout), (braw, brows, bhead, bout)):
        line = iota((ROWS, TOK), 0)
        slots = jnp.sum(jnp.where(line == MOST, head[...].astype(F32), 0.0), axis=0, keepdims=True)
        chosen = onehot((slots == line.astype(F32)) & (line < MOST))
        fresh = dot_tn(chosen, rows[...])
        mask = dot_tn(chosen, jnp.ones((ROWS, TOK), BF))
        mask = jnp.concatenate([mask] * (out.shape[1] // TOK), axis=1)
        out[...] = jnp.where(mask > 0.5, fresh, raw[...].astype(F32)).astype(BF)


def patch(fraw, frows, braw, brows):
    width = 1024
    strip = pl.BlockSpec((TOK, width), lambda i: (0, i))
    rows = pl.BlockSpec((ROWS, width), lambda i: (0, i))
    head = pl.BlockSpec((ROWS, TOK), lambda i: (0, 0))
    return pl.pallas_call(
        patch_kernel,
        grid=(D // width,),
        out_shape=(jax.ShapeDtypeStruct((TOK, D), BF),) * 2,
        in_specs=[strip, rows, head, strip, rows, head],
        out_specs=(strip, strip),
        compiler_params=pltpu.CompilerParams(vmem_limit_bytes=VMEM_LIMIT),
        name="patch",
    )(fraw, frows, frows, braw, brows, brows)


def around(value, steps):
    pairs = [(2 * z + x, 2 * ((z + steps) % NODES) + x) for z in range(NODES) for x in range(2)]
    return lax.ppermute(value, "expert", pairs)


def across_x(value):
    return lax.ppermute(value, "expert", [(e, e ^ 1) for e in range(2 * NODES)])


def section_shift(value, steps):
    count = lax.axis_size("section")
    return lax.ppermute(value, "section", [(s, (s + steps) % count) for s in range(count)])


def add(*terms):
    return functools.reduce(lambda a, b: a + b, [t.astype(F32) for t in terms]).astype(BF)


def scatter_ring(part):
    half = 48
    right = around(part[4, :half], 1)
    left = around(part[4, half:], -1)
    right = jnp.concatenate([add(part[3, :half], right), part[3, half:]])
    left = jnp.concatenate([part[5, :half], add(part[5, half:], left)])
    for k in (2, 1):
        right = add(part[k], around(right, 1))
        left = add(part[NODES - k], around(left, -1))
    total = add(part[0], around(right, 1), around(left, -1))
    return total.astype(F32) + across_x(total).astype(F32)


def activate(total):
    before = total[: 2 * MOST]
    grad = total[2 * MOST : 4 * MOST]
    hidden = jax.nn.silu(total[4 * MOST : 6 * MOST])
    sigma = jax.nn.sigmoid(before)
    pre_grad = grad * (sigma * (1.0 + before * (1.0 - sigma)))
    pad = jnp.zeros((SENT - 4 * MOST, total.shape[1]), F32)
    return jnp.concatenate([hidden, pre_grad, pad]).astype(BF)


def gather_ring(mine):
    ups, downs = [mine], [mine]
    for _ in range(3):
        ups.append(around(ups[-1], 1))
        downs.append(around(downs[-1], -1))
    head = around(ups[-1][:32], 1)
    tail = around(downs[-1][32:], -1)
    return ups[:4], (head, tail), downs[:0:-1]


def per_device(
    forward_in,
    backward_saved,
    backward_grad,
    forward_routes,
    forward_gates,
    backward_routes,
    backward_gates,
    up_weight,
    down_weight,
):
    up, down = up_weight[0], down_weight[0]
    node = (lax.axis_index("expert") // 2).astype(jnp.int32)[None]
    fraw = section_shift(forward_in[0], 1)
    braw = section_shift(backward_grad[0], -1)
    packed, kept, gate, meta = pick(
        forward_routes[0],
        forward_gates[0],
        backward_routes[0],
        backward_gates[0],
        forward_in[0],
        backward_saved[0],
        backward_grad[0],
    )
    picks = lax.all_to_all(packed, "expert", split_axis=0, concat_axis=0, tiled=True)
    part = partial_sums(node, picks, up, down)
    streams = []
    for cols in (slice(0, FIRST), slice(FIRST, FF)):
        streams.append(gather_ring(activate(scatter_ring(part[:, :, cols]))))
    (ups1, mid1, downs1), (ups2, mid2, downs2) = streams
    parts = []
    for one, two in zip(ups1, ups2):
        parts += [one, two]
    parts += [*mid1, *mid2]
    for one, two in zip(downs1, downs2):
        parts += [one, two]
    out = outward(node, up, down, parts)
    back = lax.all_to_all(out, "expert", split_axis=0, concat_axis=0, tiled=True)
    frows, brows = new_rows(back, kept, gate, meta)
    forward_out, backward_out = patch(
        fraw, section_shift(frows, 1), braw, section_shift(brows, -1)
    )
    return forward_out[None], backward_out[None]


def solution(mesh):
    row = P("section", "expert", None)
    return jax.shard_map(
        per_device,
        mesh=mesh,
        in_specs=(row, row, row, row, row, row, row, row, P("section", None, "expert")),
        out_specs=(row, row),
        check_vma=False,
    )
```

```python
import functools

import jax
import jax.numpy as jnp
from jax import lax
from jax.experimental import pallas as pl
from jax.experimental.pallas import tpu as pltpu
from jax.sharding import PartitionSpec as P

MOST = 17
TOK = 128
D = 7168
FF = 2432
COLS = 448
NODES = 8
PICK = 56
CHUNK = 104
SENT = 72
ROWS = 24
BF = jnp.bfloat16
F32 = jnp.float32
WIDE = 2 * COLS
VMEM_LIMIT = 48 * 1024 * 1024
VMEM_MOST = 60 * 1024 * 1024


def iota(shape, dim):
    return lax.broadcasted_iota(jnp.int32, shape, dim)


def dot(left, right):
    return jnp.dot(left, right, preferred_element_type=F32)


def dot_tn(left, right):
    return lax.dot_general(left, right, (((0,), (0,)), ((), ())), preferred_element_type=F32)


def dot_nt(left, right):
    return lax.dot_general(left, right, (((1,), (1,)), ((), ())), preferred_element_type=F32)


def onehot(cond):
    return jnp.where(cond, 1.0, 0.0).astype(BF)


def slot_rows(hit):
    wide = jnp.broadcast_to(hit, (TOK, TOK)).astype(BF)
    upto = onehot(iota((TOK, TOK), 0) <= iota((TOK, TOK), 1))
    return jnp.where(wide > 0.5, dot(wide, upto) - 1.0, -1.0)


def placed(slots, start):
    row = iota((PICK, TOK), 0) - start
    return (slots[:PICK] == row.astype(F32)) & (row >= 0)


def pick_kernel(place, froutes, fgates, broutes, bgates, acts, saved, cot, own, other, meta, held, sems):
    strips = 4
    width = D // strips

    def fetch(i, source):
        cols = pl.ds(i * width, width)
        ref = (acts, saved, cot)[source]
        return pltpu.make_async_copy(ref.at[:, cols], held.at[source, :, cols], sems.at[i, source])

    for i in range(strips):
        for source in range(3):
            fetch(i, source).start()

    fhits, bhits = froutes[...] == 0, broutes[...] == 0
    fslots = slot_rows(jnp.sum(jnp.where(fhits, 1.0, 0.0), axis=0, keepdims=True))
    bslots = slot_rows(jnp.sum(jnp.where(bhits, 1.0, 0.0), axis=0, keepdims=True))
    fscaling = jnp.sum(jnp.where(fhits, fgates[...], 0.0), axis=0, keepdims=True)
    bscaling = jnp.sum(jnp.where(bhits, bgates[...], 0.0), axis=0, keepdims=True)
    px = onehot(placed(fslots, 0))
    ps = onehot(placed(bslots, MOST))
    ups = placed(bslots, 2 * MOST)
    pu = onehot(ups)
    gate = jnp.sum(jnp.where(ups, bscaling, 0.0), axis=1, keepdims=True)
    hi = fscaling.astype(BF).astype(F32)
    mid = (fscaling - hi).astype(BF).astype(F32)
    low = fscaling - hi - mid
    line = iota((8, TOK), 0)
    rows = jnp.where(line == 0, fslots[:8], bslots[:8])
    for at, value in ((1, hi), (2, mid), (3, low)):
        rows = jnp.where(line == at, value, rows)
    meta[...] = rows

    first = place[1] == 0
    for j in range(NODES):
        if j % (NODES // strips) == 0:
            for source in range(3):
                fetch(j * strips // NODES, source).wait()
        cols = slice(j * WIDE, (j + 1) * WIDE)
        rows = dot(px, held[0, :, cols]) + dot(ps, held[1, :, cols]) + gate * dot(pu, held[2, :, cols])
        rows = rows.astype(BF)
        left, right = rows[:, :COLS], rows[:, COLS:]
        at = lax.rem(j + NODES - place[0], NODES)
        own[at] = jnp.where(first, left, right)
        other[at] = jnp.where(first, right, left)


def pick(place, froutes, fgates, broutes, bgates, acts, saved, cot):
    vmem = pl.BlockSpec(memory_space=pltpu.VMEM)
    anywhere = pl.BlockSpec(memory_space=pl.ANY)
    return pl.pallas_call(
        pick_kernel,
        in_specs=[pl.BlockSpec(memory_space=pltpu.SMEM)] + [vmem] * 4 + [anywhere] * 3,
        out_specs=(vmem,) * 3,
        scratch_shapes=[pltpu.VMEM((3, TOK, D), BF), pltpu.SemaphoreType.DMA((4, 3))],
        out_shape=(
            jax.ShapeDtypeStruct((NODES, PICK, COLS), BF),
            jax.ShapeDtypeStruct((NODES, PICK, COLS), BF),
            jax.ShapeDtypeStruct((8, TOK), F32),
        ),
        compiler_params=pltpu.CompilerParams(vmem_limit_bytes=VMEM_MOST),
        name="pick",
    )(place, froutes, fgates, broutes, bgates, acts, saved, cot)


def spread(owner):
    r, c = iota((CHUNK, PICK), 0), iota((CHUNK, PICK), 1)
    out = None
    for start, source in ((0, MOST), (2 * MOST, 2 * MOST), (4 * MOST, 0)):
        j = r - start - owner * MOST
        here = (j >= 0) & (j < MOST) & (c == j + source)
        out = here if out is None else out | here
    return onehot(out)


def join_kernel(place, own, other, *outs):
    mine, theirs = spread(place[1]), spread(1 - place[1])
    for k, out in enumerate(outs):
        out[...] = (dot(mine, own[k]) + dot(theirs, other[k])).astype(BF)


def join(place, own, other):
    vmem = pl.BlockSpec(memory_space=pltpu.VMEM)
    return pl.pallas_call(
        join_kernel,
        out_shape=(jax.ShapeDtypeStruct((CHUNK, COLS), BF),) * NODES,
        in_specs=[pl.BlockSpec(memory_space=pltpu.SMEM), vmem, vmem],
        out_specs=(vmem,) * NODES,
        compiler_params=pltpu.CompilerParams(vmem_limit_bytes=VMEM_LIMIT),
        name="join",
    )(place, own, other)


def partial_kernel(count, *refs):
    rows, (up, down), outs = refs[:count], refs[count : count + 2], refs[count + 2 :]
    r = iota((CHUNK, FF), 0)
    grads = (r >= 2 * MOST) & (r < 4 * MOST)
    for row, out in zip(rows, outs):
        out[...] = jnp.where(grads, dot(row[...], down[...]), dot(row[...], up[...])).astype(BF)


def partial_sums(rows, up, down):
    vmem, count = pl.BlockSpec(memory_space=pltpu.VMEM), len(rows)
    return pl.pallas_call(
        functools.partial(partial_kernel, count),
        out_shape=[jax.ShapeDtypeStruct((CHUNK, FF), BF)] * count,
        in_specs=[vmem] * (count + 2),
        out_specs=[vmem] * count,
        compiler_params=pltpu.CompilerParams(vmem_limit_bytes=VMEM_LIMIT),
        cost_estimate=pl.CostEstimate(
            flops=4 * count * CHUNK * COLS * FF, bytes_accessed=4 * COLS * FF, transcendentals=0
        ),
        name="partials",
    )(*rows, up, down)


def outward_kernel(count, *refs):
    parts, (up, down), outs = refs[:count], refs[count : count + 2], refs[count + 2 :]
    branch_rows = iota((SENT, COLS), 0) < 2 * MOST
    for part, out in zip(parts, outs):
        out[...] = jnp.where(
            branch_rows, dot_nt(part[...], down[...]), dot_nt(part[...], up[...])
        ).astype(BF)


def outward(parts, up, down):
    vmem, count = pl.BlockSpec(memory_space=pltpu.VMEM), len(parts)
    return pl.pallas_call(
        functools.partial(outward_kernel, count),
        out_shape=[jax.ShapeDtypeStruct((SENT, COLS), BF)] * count,
        in_specs=[vmem] * (count + 2),
        out_specs=[vmem] * count,
        compiler_params=pltpu.CompilerParams(vmem_limit_bytes=VMEM_LIMIT),
        cost_estimate=pl.CostEstimate(
            flops=4 * count * SENT * COLS * FF, bytes_accessed=4 * COLS * FF, transcendentals=0
        ),
        name="outward",
    )(*parts, up, down)


def settle_kernel(place, meta, *refs):
    parts, outs = refs[:NODES], refs[NODES:]
    r, c = iota((ROWS, SENT), 0), iota((ROWS, SENT), 1)
    line = iota((ROWS, COLS), 0)
    heads = []
    for rows in (((MOST, 0), (MOST + 1, 1), (MOST + 2, 2), (MOST + 3, 3)), ((MOST, 4),)):
        head = jnp.zeros((ROWS, TOK), F32)
        for at, source in rows:
            head = jnp.where(line[:, :TOK] == at, meta[source : source + 1, :], head)
        heads.append(jnp.concatenate([head, jnp.zeros((ROWS, COLS - TOK), F32)], axis=1))
    picks = []
    for start, head in ((0, heads[0]), (2 * MOST, heads[1])):
        for owner in (place[1], 1 - place[1]):
            picks.append((onehot((r < MOST) & (c == r + start + owner * MOST)), head))
    for k, part in enumerate(parts):
        at = lax.rem(place[0] + k, NODES)
        for (select, head), out in zip(picks, outs):
            out[at] = (dot(select, part[...]) + head).astype(BF)


def settle(place, meta, parts):
    vmem = pl.BlockSpec(memory_space=pltpu.VMEM)
    return pl.pallas_call(
        settle_kernel,
        out_shape=(jax.ShapeDtypeStruct((NODES, ROWS, COLS), BF),) * 4,
        in_specs=[pl.BlockSpec(memory_space=pltpu.SMEM)] + [vmem] * (NODES + 1),
        out_specs=(vmem,) * 4,
        compiler_params=pltpu.CompilerParams(vmem_limit_bytes=VMEM_LIMIT),
        name="settle",
    )(place, meta, *parts)


def patch_kernel(place, fraw, fown, fother, braw, bown, bother, fout, bout):
    first = place[1] == 0
    line = iota((ROWS, TOK), 0)
    ones = jnp.ones((ROWS, TOK), BF)
    for raw, own, other, out, scaled in (
        (fraw, fown, fother, fout, True),
        (braw, bown, bother, bout, False),
    ):
        head = own[0, :, :TOK]
        slots = jnp.sum(jnp.where(line == MOST, head.astype(F32), 0.0), axis=0, keepdims=True)
        chosen = onehot((slots == line.astype(F32)) & (line < MOST))
        if scaled:
            three = jnp.where((line > MOST) & (line < MOST + 4), head.astype(F32), 0.0).astype(BF)
            scaling = jnp.concatenate([dot_tn(three, ones)] * (WIDE // TOK), axis=1)
        for j in range(own.shape[0]):
            mine, theirs = own[j], other[j]
            rows = jnp.concatenate(
                [jnp.where(first, mine, theirs), jnp.where(first, theirs, mine)], axis=1
            )
            fresh = dot_tn(chosen, rows)
            if scaled:
                fresh = scaling * fresh
            cols = slice(j * WIDE, (j + 1) * WIDE)
            out[:, cols] = (raw[:, cols].astype(F32) + fresh).astype(BF)


def patch(place, fraw, fown, fother, braw, bown, bother):
    steps = 4
    strip = pl.BlockSpec((TOK, D // steps), lambda i: (0, i))
    rows = pl.BlockSpec((NODES // steps, ROWS, COLS), lambda i: (i, 0, 0))
    return pl.pallas_call(
        patch_kernel,
        grid=(steps,),
        out_shape=(jax.ShapeDtypeStruct((TOK, D), BF),) * 2,
        in_specs=[pl.BlockSpec(memory_space=pltpu.SMEM), strip, rows, rows, strip, rows, rows],
        out_specs=(strip, strip),
        compiler_params=pltpu.CompilerParams(vmem_limit_bytes=VMEM_LIMIT),
        name="patch",
    )(place, fraw, fown, fother, braw, bown, bother)


def around(value, steps):
    pairs = [(2 * z + x, 2 * ((z + steps) % NODES) + x) for z in range(NODES) for x in range(2)]
    return lax.ppermute(value, "expert", pairs)


def across_x(value):
    return lax.ppermute(value, "expert", [(e, e ^ 1) for e in range(2 * NODES)])


def section_shift(value, steps, flip=0):
    sections, experts = lax.axis_size("section"), lax.axis_size("expert")
    pairs = [
        (s * experts + e, (s + steps) % sections * experts + (e ^ flip))
        for s in range(sections)
        for e in range(experts)
    ]
    return lax.ppermute(value, ("section", "expert"), pairs)


def add(*terms):
    return functools.reduce(lambda a, b: a + b, [t.astype(F32) for t in terms]).astype(BF)


def scatter_ring(joined, up, down, acts, cot):
    half = 48
    came = {k: around(joined[k], k) for k in (4, 3, -3, 2, -2)}
    far, above, below = partial_sums([came[4], came[-3], came[3]], up, down)
    far, one, other = lax.optimization_barrier((far, joined[1], joined[-1]))
    right, left = around(far[:half], 1), around(far[half:], -1)
    came[1], came[-1] = around(one, 1), around(other, -1)
    right, left, came[2], came[-2] = lax.optimization_barrier((right, left, came[2], came[-2]))
    right = jnp.concatenate([add(above[:half], right), above[half:]])
    left = jnp.concatenate([below[:half], add(below[half:], left)])
    right, left, acts, cot = lax.optimization_barrier((right, left, acts, cot))
    right, left = around(right, 1), around(left, -1)
    fraw, braw = section_shift(acts, 1), section_shift(cot, -1)
    above, below = partial_sums([came[-2], came[2]], up, down)
    right, left, came[1], came[-1], above, below = lax.optimization_barrier(
        (right, left, came[1], came[-1], above, below)
    )
    right, left = around(add(above, right), 1), around(add(below, left), -1)
    above, below, mine = partial_sums([came[-1], came[1], joined[0]], up, down)
    right, left, above, below, mine = lax.optimization_barrier((right, left, above, below, mine))
    right, left = around(add(above, right), 1), around(add(below, left), -1)
    return lax.optimization_barrier((add(mine, right, left), fraw, braw))


def activate(total):
    before = total[: 2 * MOST]
    grad = total[2 * MOST : 4 * MOST]
    hidden = jax.nn.silu(total[4 * MOST : 6 * MOST])
    sigma = jax.nn.sigmoid(before)
    pre_grad = grad * (sigma * (1.0 + before * (1.0 - sigma)))
    pad = jnp.zeros((SENT - 4 * MOST, total.shape[1]), F32)
    return jnp.concatenate([hidden, pre_grad, pad]).astype(BF)


def gather_ring(mine, up, down):
    half = 32
    back = [None] * NODES
    right, left = around(mine, 1), around(mine, -1)
    made = outward([mine], up, down)
    right, left, back[0] = lax.optimization_barrier((right, left, made[0]))
    for k in (1, 2, 3):
        if k < 3:
            onward = around(right, 1), around(left, -1)
        else:
            onward = around(right[:half], 1), around(left[half:], -1)
        one, two = outward([right, left], up, down)
        back[k], back[NODES - k] = around(one, -k), around(two, k)
        if k > 1:
            onward, one, two, back[k - 1], back[NODES - k + 1] = lax.optimization_barrier(
                (onward, one, two, back[k - 1], back[NODES - k + 1])
            )
        else:
            onward, one, two = lax.optimization_barrier((onward, one, two))
        right, left = onward
    (far,) = outward([jnp.concatenate([right, left])], up, down)
    back[4] = around(far, 4)
    return back


def per_device(
    forward_in,
    backward_saved,
    backward_grad,
    forward_routes,
    forward_gates,
    backward_routes,
    backward_gates,
    up_weight,
    down_weight,
):
    up, down = up_weight[0], down_weight[0].T
    expert = lax.axis_index("expert").astype(jnp.int32)
    place = jnp.stack([expert // 2, expert % 2])
    own, other, meta = pick(
        place,
        forward_routes[0].T,
        forward_gates[0].T,
        backward_routes[0].T,
        backward_gates[0].T,
        forward_in[0],
        backward_saved[0],
        backward_grad[0],
    )
    swapped = across_x(other)
    total, fraw, braw = scatter_ring(
        join(place, own, swapped), up, down, forward_in[0], backward_grad[0]
    )
    total = total.astype(F32) + across_x(total).astype(F32)
    back = gather_ring(activate(total), up, down)
    fown, fother, bown, bother = settle(place, meta, back)
    forward_out, backward_out = patch(
        place,
        fraw,
        section_shift(fown, 1),
        section_shift(fother, 1, 1),
        braw,
        section_shift(bown, -1),
        section_shift(bother, -1, 1),
    )
    return forward_out[None], backward_out[None]


def solution(mesh):
    row = P("section", "expert", None)
    return jax.shard_map(
        per_device,
        mesh=mesh,
        in_specs=(row, row, row, row, row, row, row, row, P("section", None, "expert")),
        out_specs=(row, row),
        check_vma=False,
    )
```

```python
import functools

import jax
import jax.numpy as jnp
from jax import lax
from jax.experimental import pallas as pl
from jax.experimental.pallas import tpu as pltpu
from jax.sharding import PartitionSpec as P

MOST = 17
TOK = 128
D = 7168
FF = 2432
COLS = 448
NODES = 8
PICK = 56
CHUNK = 104
SENT = 72
ROWS = 24
SPACE = 112
FIRST = 1280
BF = jnp.bfloat16
F32 = jnp.float32
WIDE = 2 * COLS
VMEM_LIMIT = 48 * 1024 * 1024
VMEM_MOST = 60 * 1024 * 1024
STREAMS = (slice(0, FIRST), slice(FIRST, FF))
CUT = 48


def iota(shape, dim):
    return lax.broadcasted_iota(jnp.int32, shape, dim)


def dot(left, right):
    return jnp.dot(left, right, preferred_element_type=F32)


def dot_tn(left, right):
    return lax.dot_general(left, right, (((0,), (0,)), ((), ())), preferred_element_type=F32)


def dot_nt(left, right):
    return lax.dot_general(left, right, (((1,), (1,)), ((), ())), preferred_element_type=F32)


def onehot(cond):
    return jnp.where(cond, 1.0, 0.0).astype(BF)


def slot_rows(hit):
    wide = jnp.broadcast_to(hit, (TOK, TOK)).astype(BF)
    upto = onehot(iota((TOK, TOK), 0) <= iota((TOK, TOK), 1))
    return jnp.where(wide > 0.5, dot(wide, upto) - 1.0, -1.0)


def placed(slots, start):
    row = iota((PICK, TOK), 0) - start
    return (slots[:PICK] == row.astype(F32)) & (row >= 0)


def pick_kernel(froutes, fgates, broutes, bgates, acts, saved, cot, packed, meta, held, sems):
    strips = 4
    width = D // strips

    def fetch(i, source):
        cols = pl.ds(i * width, width)
        ref = (acts, saved, cot)[source]
        return pltpu.make_async_copy(ref.at[:, cols], held.at[source, :, cols], sems.at[i, source])

    for i in range(strips):
        for source in range(3):
            fetch(i, source).start()

    fhits, bhits = froutes[...] == 0, broutes[...] == 0
    fslots = slot_rows(jnp.sum(jnp.where(fhits, 1.0, 0.0), axis=0, keepdims=True))
    bslots = slot_rows(jnp.sum(jnp.where(bhits, 1.0, 0.0), axis=0, keepdims=True))
    fscaling = jnp.sum(jnp.where(fhits, fgates[...], 0.0), axis=0, keepdims=True)
    bscaling = jnp.sum(jnp.where(bhits, bgates[...], 0.0), axis=0, keepdims=True)
    px = onehot(placed(fslots, 0))
    ps = onehot(placed(bslots, MOST))
    ups = placed(bslots, 2 * MOST)
    pu = onehot(ups)
    gate = jnp.sum(jnp.where(ups, bscaling, 0.0), axis=1, keepdims=True)
    hi = fscaling.astype(BF).astype(F32)
    mid = (fscaling - hi).astype(BF).astype(F32)
    low = fscaling - hi - mid
    line = iota((8, TOK), 0)
    rows = jnp.where(line == 0, fslots[:8], bslots[:8])
    for at, value in ((1, hi), (2, mid), (3, low)):
        rows = jnp.where(line == at, value, rows)
    meta[...] = rows

    for j in range(NODES):
        if j % (NODES // strips) == 0:
            for source in range(3):
                fetch(j * strips // NODES, source).wait()
        cols = slice(j * WIDE, (j + 1) * WIDE)
        rows = dot(px, held[0, :, cols]) + dot(ps, held[1, :, cols]) + gate * dot(pu, held[2, :, cols])
        rows = rows.astype(BF)
        packed[2 * j] = rows[:, :COLS]
        packed[2 * j + 1] = rows[:, COLS:]


def pick(froutes, fgates, broutes, bgates, acts, saved, cot):
    vmem = pl.BlockSpec(memory_space=pltpu.VMEM)
    anywhere = pl.BlockSpec(memory_space=pl.ANY)
    return pl.pallas_call(
        pick_kernel,
        in_specs=[vmem] * 4 + [anywhere] * 3,
        out_specs=(vmem,) * 2,
        scratch_shapes=[pltpu.VMEM((3, TOK, D), BF), pltpu.SemaphoreType.DMA((4, 3))],
        out_shape=(
            jax.ShapeDtypeStruct((2 * NODES, PICK, COLS), BF),
            jax.ShapeDtypeStruct((8, TOK), F32),
        ),
        compiler_params=pltpu.CompilerParams(vmem_limit_bytes=VMEM_MOST),
        name="pick",
    )(froutes, fgates, broutes, bgates, acts, saved, cot)


def spread(owner):
    r, c = iota((CHUNK, PICK), 0), iota((CHUNK, PICK), 1)
    out = None
    for start, source in ((0, MOST), (2 * MOST, 2 * MOST), (4 * MOST, 0)):
        j = r - start - owner * MOST
        here = (j >= 0) & (j < MOST) & (c == j + source)
        out = here if out is None else out | here
    return onehot(out)


def partial_kernel(place, picks, up, down, *refs):
    far, sums, big = refs[:4], refs[4:6], refs[6]
    e0, e1 = spread(0), spread(1)
    group = 4
    for base in range(0, NODES, group):
        for k in range(base, base + group):
            at = 2 * lax.rem(place[0] + k, NODES)
            value = dot(e0, picks[at]) + dot(e1, picks[at + 1])
            big[pl.ds((k - base) * SPACE, CHUNK), :] = value.astype(BF)
        rows = big[...]
        for i, cols in enumerate(STREAMS):
            ups, downs = dot(rows, up[:, cols]), dot(rows, down[:, cols])
            for k in range(base, base + group):
                mine = slice((k - base) * SPACE, (k - base) * SPACE + CHUNK)
                r = iota((CHUNK, cols.stop - cols.start), 0)
                grads = (r >= 2 * MOST) & (r < 4 * MOST)
                value = jnp.where(grads, downs[mine], ups[mine]).astype(BF)
                if k == 4:
                    far[2 * i][...] = value[:CUT]
                    far[2 * i + 1][...] = value[CUT:]
                else:
                    sums[i][k if k < 4 else k - 1] = value


def partial_sums(place, picks, up, down):
    vmem = pl.BlockSpec(memory_space=pltpu.VMEM)
    widths = [cols.stop - cols.start for cols in STREAMS]
    shapes = [jax.ShapeDtypeStruct((rows, w), BF) for w in widths for rows in (CUT, CHUNK - CUT)]
    shapes += [jax.ShapeDtypeStruct((NODES - 1, CHUNK, w), BF) for w in widths]
    return pl.pallas_call(
        partial_kernel,
        out_shape=shapes,
        in_specs=[pl.BlockSpec(memory_space=pltpu.SMEM)] + [vmem] * 3,
        out_specs=[vmem] * len(shapes),
        scratch_shapes=[pltpu.VMEM((4 * SPACE, COLS), BF)],
        compiler_params=pltpu.CompilerParams(vmem_limit_bytes=VMEM_LIMIT),
        name="partials",
    )(place, picks, up, down)


def outward_kernel(count, *refs):
    parts, (up, down), outs = refs[:count], refs[count : count + 2], refs[count + 2 :]
    branch_rows = iota((SENT, COLS), 0) < 2 * MOST
    for part, out in zip(parts, outs):
        out[...] = jnp.where(
            branch_rows, dot_nt(part[...], down[...]), dot_nt(part[...], up[...])
        ).astype(BF)


def outward(parts, up, down):
    vmem, count = pl.BlockSpec(memory_space=pltpu.VMEM), len(parts)
    return pl.pallas_call(
        functools.partial(outward_kernel, count),
        out_shape=[jax.ShapeDtypeStruct((SENT, COLS), BF)] * count,
        in_specs=[vmem] * (count + 2),
        out_specs=[vmem] * count,
        compiler_params=pltpu.CompilerParams(vmem_limit_bytes=VMEM_LIMIT),
        cost_estimate=pl.CostEstimate(
            flops=4 * count * SENT * COLS * FF, bytes_accessed=4 * COLS * FF, transcendentals=0
        ),
        name="outward",
    )(*parts, up, down)


def settle_kernel(place, meta, *refs):
    parts, outs = refs[:NODES], refs[NODES:]
    r, c = iota((ROWS, SENT), 0), iota((ROWS, SENT), 1)
    line = iota((ROWS, COLS), 0)
    heads = []
    for rows in (((MOST, 0), (MOST + 1, 1), (MOST + 2, 2), (MOST + 3, 3)), ((MOST, 4),)):
        head = jnp.zeros((ROWS, TOK), F32)
        for at, source in rows:
            head = jnp.where(line[:, :TOK] == at, meta[source : source + 1, :], head)
        heads.append(jnp.concatenate([head, jnp.zeros((ROWS, COLS - TOK), F32)], axis=1))
    picks = []
    for start, head in ((0, heads[0]), (2 * MOST, heads[1])):
        for owner in (place[1], 1 - place[1]):
            picks.append((onehot((r < MOST) & (c == r + start + owner * MOST)), head))
    for k, part in enumerate(parts):
        at = lax.rem(place[0] + k, NODES)
        for (select, head), out in zip(picks, outs):
            out[at] = (dot(select, part[...]) + head).astype(BF)


def settle(place, meta, parts):
    vmem = pl.BlockSpec(memory_space=pltpu.VMEM)
    return pl.pallas_call(
        settle_kernel,
        out_shape=(jax.ShapeDtypeStruct((NODES, ROWS, COLS), BF),) * 4,
        in_specs=[pl.BlockSpec(memory_space=pltpu.SMEM)] + [vmem] * (NODES + 1),
        out_specs=(vmem,) * 4,
        compiler_params=pltpu.CompilerParams(vmem_limit_bytes=VMEM_LIMIT),
        name="settle",
    )(place, meta, *parts)


def patch_kernel(place, fraw, fown, fother, braw, bown, bother, fout, bout):
    first = place[1] == 0
    line = iota((ROWS, TOK), 0)
    ones = jnp.ones((ROWS, TOK), BF)
    for raw, own, other, out, scaled in (
        (fraw, fown, fother, fout, True),
        (braw, bown, bother, bout, False),
    ):
        head = own[0, :, :TOK]
        slots = jnp.sum(jnp.where(line == MOST, head.astype(F32), 0.0), axis=0, keepdims=True)
        chosen = onehot((slots == line.astype(F32)) & (line < MOST))
        if scaled:
            three = jnp.where((line > MOST) & (line < MOST + 4), head.astype(F32), 0.0).astype(BF)
            scaling = jnp.concatenate([dot_tn(three, ones)] * (WIDE // TOK), axis=1)
        for j in range(own.shape[0]):
            mine, theirs = own[j], other[j]
            rows = jnp.concatenate(
                [jnp.where(first, mine, theirs), jnp.where(first, theirs, mine)], axis=1
            )
            fresh = dot_tn(chosen, rows)
            if scaled:
                fresh = scaling * fresh
            cols = slice(j * WIDE, (j + 1) * WIDE)
            out[:, cols] = (raw[:, cols].astype(F32) + fresh).astype(BF)


def patch(place, fraw, fown, fother, braw, bown, bother):
    steps = 4
    strip = pl.BlockSpec((TOK, D // steps), lambda i: (0, i))
    rows = pl.BlockSpec((NODES // steps, ROWS, COLS), lambda i: (i, 0, 0))
    return pl.pallas_call(
        patch_kernel,
        grid=(steps,),
        out_shape=(jax.ShapeDtypeStruct((TOK, D), BF),) * 2,
        in_specs=[pl.BlockSpec(memory_space=pltpu.SMEM), strip, rows, rows, strip, rows, rows],
        out_specs=(strip, strip),
        compiler_params=pltpu.CompilerParams(vmem_limit_bytes=VMEM_LIMIT),
        name="patch",
    )(place, fraw, fown, fother, braw, bown, bother)


def around(value, steps):
    pairs = [(2 * z + x, 2 * ((z + steps) % NODES) + x) for z in range(NODES) for x in range(2)]
    return lax.ppermute(value, "expert", pairs)


def across_x(value):
    return lax.ppermute(value, "expert", [(e, e ^ 1) for e in range(2 * NODES)])


def section_shift(value, steps, flip=0):
    sections, experts = lax.axis_size("section"), lax.axis_size("expert")
    pairs = [
        (s * experts + e, (s + steps) % sections * experts + (e ^ flip))
        for s in range(sections)
        for e in range(experts)
    ]
    return lax.ppermute(value, ("section", "expert"), pairs)


def add(*terms):
    return functools.reduce(lambda a, b: a + b, [t.astype(F32) for t in terms]).astype(BF)


def scatter_ring(right, left, part):
    right, left = around(right, 1), around(left, -1)
    right = jnp.concatenate([add(part[3, :CUT], right), part[3, CUT:]])
    left = jnp.concatenate([part[4, :CUT], add(part[4, CUT:], left)])
    for k in (2, 1):
        right = add(part[k], around(right, 1))
        left = add(part[NODES - 1 - k], around(left, -1))
    total = add(part[0], around(right, 1), around(left, -1))
    return total.astype(F32) + across_x(total).astype(F32)


def activate(total):
    before = total[: 2 * MOST]
    grad = total[2 * MOST : 4 * MOST]
    hidden = jax.nn.silu(total[4 * MOST : 6 * MOST])
    sigma = jax.nn.sigmoid(before)
    pre_grad = grad * (sigma * (1.0 + before * (1.0 - sigma)))
    pad = jnp.zeros((SENT - 4 * MOST, total.shape[1]), F32)
    return jnp.concatenate([hidden, pre_grad, pad]).astype(BF)


def gather_ring(mine, up, down):
    half = 32
    back = [None] * NODES
    right, left = around(mine, 1), around(mine, -1)
    made = outward([mine], up, down)
    right, left, back[0] = lax.optimization_barrier((right, left, made[0]))
    for k in (1, 2, 3):
        if k < 3:
            onward = around(right, 1), around(left, -1)
        else:
            onward = around(right[:half], 1), around(left[half:], -1)
        one, two = outward([right, left], up, down)
        back[k], back[NODES - k] = around(one, -k), around(two, k)
        if k > 1:
            onward, one, two, back[k - 1], back[NODES - k + 1] = lax.optimization_barrier(
                (onward, one, two, back[k - 1], back[NODES - k + 1])
            )
        else:
            onward, one, two = lax.optimization_barrier((onward, one, two))
        right, left = onward
    (far,) = outward([jnp.concatenate([right, left])], up, down)
    back[4] = around(far, 4)
    return back


def per_device(
    forward_in,
    backward_saved,
    backward_grad,
    forward_routes,
    forward_gates,
    backward_routes,
    backward_gates,
    up_weight,
    down_weight,
):
    up, down = up_weight[0], down_weight[0].T
    expert = lax.axis_index("expert").astype(jnp.int32)
    place = jnp.stack([expert // 2, expert % 2])
    packed, meta = pick(
        forward_routes[0].T,
        forward_gates[0].T,
        backward_routes[0].T,
        backward_gates[0].T,
        forward_in[0],
        backward_saved[0],
        backward_grad[0],
    )
    packed, acts, cot = lax.optimization_barrier((packed, forward_in[0], backward_grad[0]))
    picks = lax.all_to_all(packed, "expert", split_axis=0, concat_axis=0, tiled=True)
    fraw, braw = section_shift(acts, 1), section_shift(cot, -1)
    picks, fraw, braw = lax.optimization_barrier((picks, fraw, braw))
    right1, left1, right2, left2, part1, part2 = partial_sums(place, picks, up, down)
    totals = [scatter_ring(right1, left1, part1), scatter_ring(right2, left2, part2)]
    mine = jnp.concatenate([activate(total) for total in totals], axis=1)
    back = gather_ring(mine, up, down)
    fown, fother, bown, bother = settle(place, meta, back)
    forward_out, backward_out = patch(
        place,
        fraw,
        section_shift(fown, 1),
        section_shift(fother, 1, 1),
        braw,
        section_shift(bown, -1),
        section_shift(bother, -1, 1),
    )
    return forward_out[None], backward_out[None]


def solution(mesh):
    row = P("section", "expert", None)
    return jax.shard_map(
        per_device,
        mesh=mesh,
        in_specs=(row, row, row, row, row, row, row, row, P("section", None, "expert")),
        out_specs=(row, row),
        check_vma=False,
    )
```

```python
import functools

import jax
import jax.numpy as jnp
from jax import lax
from jax.experimental import pallas as pl
from jax.experimental.pallas import tpu as pltpu
from jax.sharding import PartitionSpec as P

MOST = 17
TOK = 128
D = 7168
FF = 2432
COLS = 448
NODES = 8
PICK = 56
CHUNK = 104
SENT = 72
ROWS = 24
FIRST = 1280
BF = jnp.bfloat16
F32 = jnp.float32
WIDE = 2 * COLS
VMEM_LIMIT = 48 * 1024 * 1024
VMEM_MOST = 60 * 1024 * 1024
STREAMS = (slice(0, FIRST), slice(FIRST, FF))
CUT = 48


def iota(shape, dim):
    return lax.broadcasted_iota(jnp.int32, shape, dim)


def dot(left, right):
    return jnp.dot(left, right, preferred_element_type=F32)


def dot_tn(left, right):
    return lax.dot_general(left, right, (((0,), (0,)), ((), ())), preferred_element_type=F32)


def dot_nt(left, right):
    return lax.dot_general(left, right, (((1,), (1,)), ((), ())), preferred_element_type=F32)


def onehot(cond):
    return jnp.where(cond, 1.0, 0.0).astype(BF)


def slot_rows(hit):
    wide = jnp.broadcast_to(hit, (TOK, TOK)).astype(BF)
    upto = onehot(iota((TOK, TOK), 0) <= iota((TOK, TOK), 1))
    return jnp.where(wide > 0.5, dot(wide, upto) - 1.0, -1.0)


def placed(slots, start):
    row = iota((PICK, TOK), 0) - start
    return (slots[:PICK] == row.astype(F32)) & (row >= 0)


def pick_kernel(froutes, fgates, broutes, bgates, acts, saved, cot, packed, meta, held, sems):
    sources = (acts, saved, cot)

    def strip(j):
        return pl.ds(pl.multiple_of(j * WIDE, TOK), WIDE)

    def fetch(j, i):
        return pltpu.make_async_copy(
            sources[i].at[:, strip(j)], held.at[i, :, strip(j)], sems.at[j, i]
        )

    @pl.loop(0, NODES)
    def _(j):
        for i in range(3):
            fetch(j, i).start()

    fhits, bhits = froutes[...] == 0, broutes[...] == 0
    fslots = slot_rows(jnp.sum(jnp.where(fhits, 1.0, 0.0), axis=0, keepdims=True))
    bslots = slot_rows(jnp.sum(jnp.where(bhits, 1.0, 0.0), axis=0, keepdims=True))
    fscaling = jnp.sum(jnp.where(fhits, fgates[...], 0.0), axis=0, keepdims=True)
    bscaling = jnp.sum(jnp.where(bhits, bgates[...], 0.0), axis=0, keepdims=True)
    px = onehot(placed(fslots, 0))
    ps = onehot(placed(bslots, MOST))
    ups = placed(bslots, 2 * MOST)
    pu = onehot(ups)
    gate = jnp.sum(jnp.where(ups, bscaling, 0.0), axis=1, keepdims=True)
    hi = fscaling.astype(BF).astype(F32)
    mid = (fscaling - hi).astype(BF).astype(F32)
    low = fscaling - hi - mid
    line = iota((8, TOK), 0)
    rows = jnp.where(line == 0, fslots[:8], bslots[:8])
    for at, value in ((1, hi), (2, mid), (3, low)):
        rows = jnp.where(line == at, value, rows)
    meta[...] = rows

    @pl.loop(0, NODES)
    def _(j):
        for i in range(3):
            fetch(j, i).wait()
        x, saves, raw = (held[i, :, strip(j)] for i in range(3))
        rows = (dot(px, x) + dot(ps, saves) + gate * dot(pu, raw)).astype(BF)
        packed[2 * j] = rows[:, :COLS]
        packed[2 * j + 1] = rows[:, COLS:]


def pick(froutes, fgates, broutes, bgates, acts, saved, cot):
    vmem = pl.BlockSpec(memory_space=pltpu.VMEM)
    anywhere = pl.BlockSpec(memory_space=pl.ANY)
    return pl.pallas_call(
        pick_kernel,
        in_specs=[vmem] * 4 + [anywhere] * 3,
        out_specs=(vmem,) * 2,
        scratch_shapes=[pltpu.VMEM((3, TOK, D), BF), pltpu.SemaphoreType.DMA((NODES, 3))],
        out_shape=(
            jax.ShapeDtypeStruct((2 * NODES, PICK, COLS), BF),
            jax.ShapeDtypeStruct((8, TOK), F32),
        ),
        compiler_params=pltpu.CompilerParams(vmem_limit_bytes=VMEM_MOST),
        name="pick",
    )(froutes, fgates, broutes, bgates, acts, saved, cot)


def spread(rows, places):
    r, c = iota((rows, PICK), 0), iota((rows, PICK), 1)
    out = None
    for start, source in places:
        j = r - start
        here = (j >= 0) & (j < MOST) & (c == j + source)
        out = here if out is None else out | here
    return onehot(out)


def partial_kernel(place, picks, up, down, *refs):
    far, sums = refs[:4], refs[4:6]
    tall, low = 72, 40
    edge = 4 * MOST - 64
    inputs, grads = [], []
    for half in range(2):
        for owner in range(2):
            at = half * tall + owner * MOST
            inputs.append(spread(2 * tall + 8, ((at, MOST), (at + 2 * MOST, 0))))
            grads.append(spread(2 * low, ((half * low + edge + owner * MOST, 2 * MOST),)))

    @pl.loop(0, NODES // 2)
    def _(pair):
        blocks = []
        for half in range(2):
            at = 2 * lax.rem(place[0] + 2 * pair + half, NODES)
            blocks += [picks[at], picks[at + 1]]
        rows = sum(dot(e, block) for e, block in zip(inputs, blocks)).astype(BF)
        ends = sum(dot(e, block) for e, block in zip(grads, blocks)).astype(BF)
        for out, cols in zip(sums, STREAMS):
            ups, downs = dot(rows, up[:, cols]), dot(ends, down[:, cols])
            first = iota((16, cols.stop - cols.start), 0) < edge
            for half in range(2):
                k, i, j = 2 * pair + half, half * tall, half * low
                out[k, :64, :] = ups[i : i + 64].astype(BF)
                mixed = jnp.where(first, ups[i + 64 : i + 80], downs[j : j + 16])
                out[k, 64:80, :] = mixed.astype(BF)
                out[k, 80:, :] = downs[j + 16 : j + low].astype(BF)

    for i, out in enumerate(sums):
        value = out[4]
        far[2 * i][...] = value[:CUT]
        far[2 * i + 1][...] = value[CUT:]


def partial_sums(place, picks, up, down):
    vmem = pl.BlockSpec(memory_space=pltpu.VMEM)
    widths = [cols.stop - cols.start for cols in STREAMS]
    shapes = [jax.ShapeDtypeStruct((rows, w), BF) for w in widths for rows in (CUT, CHUNK - CUT)]
    shapes += [jax.ShapeDtypeStruct((NODES, CHUNK, w), BF) for w in widths]
    return pl.pallas_call(
        partial_kernel,
        out_shape=shapes,
        in_specs=[pl.BlockSpec(memory_space=pltpu.SMEM)] + [vmem] * 3,
        out_specs=[vmem] * len(shapes),
        compiler_params=pltpu.CompilerParams(vmem_limit_bytes=VMEM_LIMIT),
        name="partials",
    )(place, picks, up, down)


def outward_kernel(count, *refs):
    parts, (up, down) = refs[:count], refs[count : count + 2]
    outs, (hold, made) = refs[count + 2 : -2], refs[-2:]
    for i, part in enumerate(parts):
        hold[i] = part[...]

    @pl.loop(0, count)
    def _(i):
        rows = hold[i]
        branch, back = dot_nt(rows[:48], down[...]), dot_nt(rows[32:], up[...])
        made[i, :32, :] = branch[:32].astype(BF)
        line = iota((16, COLS), 0)
        made[i, 32:48, :] = jnp.where(line < 2, branch[32:], back[:16]).astype(BF)
        made[i, 48:, :] = back[16:].astype(BF)

    for i, out in enumerate(outs):
        out[...] = made[i]


def outward(parts, up, down):
    vmem, count = pl.BlockSpec(memory_space=pltpu.VMEM), len(parts)
    return pl.pallas_call(
        functools.partial(outward_kernel, count),
        out_shape=[jax.ShapeDtypeStruct((SENT, COLS), BF)] * count,
        in_specs=[vmem] * (count + 2),
        out_specs=[vmem] * count,
        scratch_shapes=[pltpu.VMEM((count, SENT, FF), BF), pltpu.VMEM((count, SENT, COLS), BF)],
        compiler_params=pltpu.CompilerParams(vmem_limit_bytes=VMEM_LIMIT),
        cost_estimate=pl.CostEstimate(
            flops=4 * count * SENT * COLS * FF, bytes_accessed=4 * COLS * FF, transcendentals=0
        ),
        name="outward",
    )(*parts, up, down)


def settle_kernel(place, meta, *refs):
    parts, outs, held = refs[:NODES], refs[NODES:-1], refs[-1]
    for k, part in enumerate(parts):
        held[k] = part[...]
    r, c = iota((ROWS, SENT), 0), iota((ROWS, SENT), 1)
    line = iota((ROWS, COLS), 0)
    heads = []
    for rows in (((MOST, 0), (MOST + 1, 1), (MOST + 2, 2), (MOST + 3, 3)), ((MOST, 4),)):
        head = jnp.zeros((ROWS, TOK), F32)
        for at, source in rows:
            head = jnp.where(line[:, :TOK] == at, meta[source : source + 1, :], head)
        heads.append(jnp.concatenate([head, jnp.zeros((ROWS, COLS - TOK), F32)], axis=1))
    picks = []
    for start, head in ((0, heads[0]), (2 * MOST, heads[1])):
        for owner in (place[1], 1 - place[1]):
            picks.append((onehot((r < MOST) & (c == r + start + owner * MOST)), head))

    @pl.loop(0, NODES)
    def _(k):
        at = lax.rem(place[0] + k, NODES)
        rows = held[k]
        for (select, head), out in zip(picks, outs):
            out[at] = (dot(select, rows) + head).astype(BF)


def settle(place, meta, parts):
    vmem = pl.BlockSpec(memory_space=pltpu.VMEM)
    return pl.pallas_call(
        settle_kernel,
        out_shape=(jax.ShapeDtypeStruct((NODES, ROWS, COLS), BF),) * 4,
        in_specs=[pl.BlockSpec(memory_space=pltpu.SMEM)] + [vmem] * (NODES + 1),
        out_specs=(vmem,) * 4,
        scratch_shapes=[pltpu.VMEM((NODES, SENT, COLS), BF)],
        compiler_params=pltpu.CompilerParams(vmem_limit_bytes=VMEM_LIMIT),
        name="settle",
    )(place, meta, *parts)


def patch_kernel(place, fraw, fown, fother, braw, bown, bother, fout, bout):
    first = place[1] == 0
    line = iota((ROWS, TOK), 0)
    ones = jnp.ones((ROWS, TOK), BF)
    for raw, own, other, out, scaled in (
        (fraw, fown, fother, fout, True),
        (braw, bown, bother, bout, False),
    ):
        head = own[0, :, :TOK]
        slots = jnp.sum(jnp.where(line == MOST, head.astype(F32), 0.0), axis=0, keepdims=True)
        chosen = onehot((slots == line.astype(F32)) & (line < MOST))
        if scaled:
            three = jnp.where((line > MOST) & (line < MOST + 4), head.astype(F32), 0.0).astype(BF)
            scaling = jnp.concatenate([dot_tn(three, ones)] * (WIDE // TOK), axis=1)
        for j in range(own.shape[0]):
            mine, theirs = own[j], other[j]
            rows = jnp.concatenate(
                [jnp.where(first, mine, theirs), jnp.where(first, theirs, mine)], axis=1
            )
            fresh = dot_tn(chosen, rows)
            if scaled:
                fresh = scaling * fresh
            cols = slice(j * WIDE, (j + 1) * WIDE)
            out[:, cols] = (raw[:, cols].astype(F32) + fresh).astype(BF)


def patch(place, fraw, fown, fother, braw, bown, bother):
    steps = 4
    strip = pl.BlockSpec((TOK, D // steps), lambda i: (0, i))
    rows = pl.BlockSpec((NODES // steps, ROWS, COLS), lambda i: (i, 0, 0))
    return pl.pallas_call(
        patch_kernel,
        grid=(steps,),
        out_shape=(jax.ShapeDtypeStruct((TOK, D), BF),) * 2,
        in_specs=[pl.BlockSpec(memory_space=pltpu.SMEM), strip, rows, rows, strip, rows, rows],
        out_specs=(strip, strip),
        compiler_params=pltpu.CompilerParams(vmem_limit_bytes=VMEM_LIMIT),
        name="patch",
    )(place, fraw, fown, fother, braw, bown, bother)


def around(value, steps):
    pairs = [(2 * z + x, 2 * ((z + steps) % NODES) + x) for z in range(NODES) for x in range(2)]
    return lax.ppermute(value, "expert", pairs)


def across_x(value):
    return lax.ppermute(value, "expert", [(e, e ^ 1) for e in range(2 * NODES)])


def section_shift(value, steps, flip=0):
    sections, experts = lax.axis_size("section"), lax.axis_size("expert")
    pairs = [
        (s * experts + e, (s + steps) % sections * experts + (e ^ flip))
        for s in range(sections)
        for e in range(experts)
    ]
    return lax.ppermute(value, ("section", "expert"), pairs)


def add(*terms):
    return functools.reduce(lambda a, b: a + b, [t.astype(F32) for t in terms]).astype(BF)


def scatter_ring(right, left, part):
    right, left = around(right, 1), around(left, -1)
    right = jnp.concatenate([add(part[3, :CUT], right), part[3, CUT:]])
    left = jnp.concatenate([part[5, :CUT], add(part[5, CUT:], left)])
    for k in (2, 1):
        right = add(part[k], around(right, 1))
        left = add(part[NODES - k], around(left, -1))
    total = add(part[0], around(right, 1), around(left, -1))
    return total.astype(F32) + across_x(total).astype(F32)


def activate(total):
    before = total[: 2 * MOST]
    hidden = jax.nn.silu(total[2 * MOST : 4 * MOST])
    grad = total[4 * MOST : 6 * MOST]
    sigma = jax.nn.sigmoid(before)
    pre_grad = grad * (sigma * (1.0 + before * (1.0 - sigma)))
    pad = jnp.zeros((SENT - 4 * MOST, total.shape[1]), F32)
    return jnp.concatenate([hidden, pre_grad, pad]).astype(BF)


def gather_ring(mine, up, down):
    half = 32
    back = [None] * NODES
    right, left = around(mine, 1), around(mine, -1)
    made = outward([mine], up, down)
    right, left, back[0] = lax.optimization_barrier((right, left, made[0]))
    for k in (1, 2, 3):
        if k < 3:
            onward = around(right, 1), around(left, -1)
        else:
            onward = around(right[:half], 1), around(left[half:], -1)
        one, two = outward([right, left], up, down)
        back[k], back[NODES - k] = around(one, -k), around(two, k)
        if k > 1:
            onward, one, two, back[k - 1], back[NODES - k + 1] = lax.optimization_barrier(
                (onward, one, two, back[k - 1], back[NODES - k + 1])
            )
        else:
            onward, one, two = lax.optimization_barrier((onward, one, two))
        right, left = onward
    (far,) = outward([jnp.concatenate([right, left])], up, down)
    back[4] = around(far, 4)
    return back


def per_device(
    forward_in,
    backward_saved,
    backward_grad,
    forward_routes,
    forward_gates,
    backward_routes,
    backward_gates,
    up_weight,
    down_weight,
):
    up, down = up_weight[0], down_weight[0].T
    expert = lax.axis_index("expert").astype(jnp.int32)
    place = jnp.stack([expert // 2, expert % 2])
    packed, meta = pick(
        forward_routes[0].T,
        forward_gates[0].T,
        backward_routes[0].T,
        backward_gates[0].T,
        forward_in[0],
        backward_saved[0],
        backward_grad[0],
    )
    packed, acts, cot = lax.optimization_barrier((packed, forward_in[0], backward_grad[0]))
    picks = lax.all_to_all(packed, "expert", split_axis=0, concat_axis=0, tiled=True)
    fraw, braw = section_shift(acts, 1), section_shift(cot, -1)
    (right1, left1, right2, left2, part1, part2), fraw, braw = lax.optimization_barrier(
        (partial_sums(place, picks, up, down), fraw, braw)
    )
    totals = [scatter_ring(right1, left1, part1), scatter_ring(right2, left2, part2)]
    mine = jnp.concatenate([activate(total) for total in totals], axis=1)
    back = gather_ring(mine, up, down)
    fown, fother, bown, bother = settle(place, meta, back)
    forward_out, backward_out = patch(
        place,
        fraw,
        section_shift(fown, 1),
        section_shift(fother, 1, 1),
        braw,
        section_shift(bown, -1),
        section_shift(bother, -1, 1),
    )
    return forward_out[None], backward_out[None]


def solution(mesh):
    row = P("section", "expert", None)
    return jax.shard_map(
        per_device,
        mesh=mesh,
        in_specs=(row, row, row, row, row, row, row, row, P("section", None, "expert")),
        out_specs=(row, row),
        check_vma=False,
    )
```

```python
import functools

import jax
import jax.numpy as jnp
from jax import lax
from jax.experimental import pallas as pl
from jax.experimental.pallas import tpu as pltpu
from jax.sharding import PartitionSpec as P

MOST = 17
TOK = 128
D = 7168
FF = 2432
COLS = 448
NODES = 8
PICK = 56
CHUNK = 104
SENT = 72
ROWS = 24
FIRST = 1280
BF = jnp.bfloat16
F32 = jnp.float32
WIDE = 2 * COLS
VMEM_LIMIT = 24 * 1024 * 1024
VMEM_MOST = 60 * 1024 * 1024
STREAMS = (slice(0, FIRST), slice(FIRST, FF))
CUT = 48


def iota(shape, dim):
    return lax.broadcasted_iota(jnp.int32, shape, dim)


def dot(left, right):
    return jnp.dot(left, right, preferred_element_type=F32)


def dot_tn(left, right):
    return lax.dot_general(left, right, (((0,), (0,)), ((), ())), preferred_element_type=F32)


def dot_nt(left, right):
    return lax.dot_general(left, right, (((1,), (1,)), ((), ())), preferred_element_type=F32)


def onehot(cond):
    return jnp.where(cond, 1.0, 0.0).astype(BF)


def slot_rows(hit):
    wide = jnp.broadcast_to(hit, (TOK, TOK)).astype(BF)
    upto = onehot(iota((TOK, TOK), 0) <= iota((TOK, TOK), 1))
    return jnp.where(wide > 0.5, dot(wide, upto) - 1.0, -1.0)


def placed(slots, start):
    row = iota((PICK, TOK), 0) - start
    return (slots[:PICK] == row.astype(F32)) & (row >= 0)


def pick_kernel(froutes, fgates, broutes, bgates, acts, saved, cot, packed, meta, held, sems):
    sources = (acts, saved, cot)

    def strip(j):
        return pl.ds(pl.multiple_of(j * WIDE, TOK), WIDE)

    def fetch(j, i):
        return pltpu.make_async_copy(
            sources[i].at[:, strip(j)], held.at[i, :, strip(j)], sems.at[j, i]
        )

    @pl.loop(0, NODES)
    def _(j):
        for i in range(3):
            fetch(j, i).start()

    fhits, bhits = froutes[...] == 0, broutes[...] == 0
    fslots = slot_rows(jnp.sum(jnp.where(fhits, 1.0, 0.0), axis=0, keepdims=True))
    bslots = slot_rows(jnp.sum(jnp.where(bhits, 1.0, 0.0), axis=0, keepdims=True))
    fscaling = jnp.sum(jnp.where(fhits, fgates[...], 0.0), axis=0, keepdims=True)
    bscaling = jnp.sum(jnp.where(bhits, bgates[...], 0.0), axis=0, keepdims=True)
    px = onehot(placed(fslots, 0))
    ps = onehot(placed(bslots, MOST))
    ups = placed(bslots, 2 * MOST)
    pu = onehot(ups)
    gate = jnp.sum(jnp.where(ups, bscaling, 0.0), axis=1, keepdims=True)
    hi = fscaling.astype(BF).astype(F32)
    mid = (fscaling - hi).astype(BF).astype(F32)
    low = fscaling - hi - mid
    line = iota((8, TOK), 0)
    rows = jnp.where(line == 0, fslots[:8], bslots[:8])
    for at, value in ((1, hi), (2, mid), (3, low)):
        rows = jnp.where(line == at, value, rows)
    meta[...] = rows

    @pl.loop(0, NODES)
    def _(j):
        for i in range(3):
            fetch(j, i).wait()
        x, saves, raw = (held[i, :, strip(j)] for i in range(3))
        rows = (dot(px, x) + dot(ps, saves) + gate * dot(pu, raw)).astype(BF)
        packed[2 * j] = rows[:, :COLS]
        packed[2 * j + 1] = rows[:, COLS:]


def pick(froutes, fgates, broutes, bgates, acts, saved, cot):
    vmem = pl.BlockSpec(memory_space=pltpu.VMEM)
    anywhere = pl.BlockSpec(memory_space=pl.ANY)
    return pl.pallas_call(
        pick_kernel,
        in_specs=[vmem] * 4 + [anywhere] * 3,
        out_specs=(vmem,) * 2,
        scratch_shapes=[pltpu.VMEM((3, TOK, D), BF), pltpu.SemaphoreType.DMA((NODES, 3))],
        out_shape=(
            jax.ShapeDtypeStruct((2 * NODES, PICK, COLS), BF),
            jax.ShapeDtypeStruct((8, TOK), F32),
        ),
        compiler_params=pltpu.CompilerParams(vmem_limit_bytes=VMEM_MOST),
        name="pick",
    )(froutes, fgates, broutes, bgates, acts, saved, cot)


def spread(rows, places):
    r, c = iota((rows, PICK), 0), iota((rows, PICK), 1)
    out = None
    for start, source in places:
        j = r - start
        here = (j >= 0) & (j < MOST) & (c == j + source)
        out = here if out is None else out | here
    return onehot(out)


def partial_kernel(place, picks, up, down, *refs):
    far, sums = refs[:4], refs[4:6]
    tall, low = 72, 40
    edge = 4 * MOST - 64
    inputs, grads = [], []
    for half in range(2):
        for owner in range(2):
            at = half * tall + owner * MOST
            inputs.append(spread(2 * tall + 8, ((at, MOST), (at + 2 * MOST, 0))))
            grads.append(spread(2 * low, ((half * low + edge + owner * MOST, 2 * MOST),)))

    @pl.loop(0, NODES // 2)
    def _(pair):
        blocks = []
        for half in range(2):
            at = 2 * lax.rem(place[0] + 2 * pair + half, NODES)
            blocks += [picks[at], picks[at + 1]]
        rows = sum(dot(e, block) for e, block in zip(inputs, blocks)).astype(BF)
        ends = sum(dot(e, block) for e, block in zip(grads, blocks)).astype(BF)
        for out, cols in zip(sums, STREAMS):
            ups, downs = dot(rows, up[:, cols]), dot(ends, down[:, cols])
            first = iota((16, cols.stop - cols.start), 0) < edge
            for half in range(2):
                k, i, j = 2 * pair + half, half * tall, half * low
                out[k, :64, :] = ups[i : i + 64].astype(BF)
                mixed = jnp.where(first, ups[i + 64 : i + 80], downs[j : j + 16])
                out[k, 64:80, :] = mixed.astype(BF)
                out[k, 80:, :] = downs[j + 16 : j + low].astype(BF)

    for i, out in enumerate(sums):
        value = out[4]
        far[2 * i][...] = value[:CUT]
        far[2 * i + 1][...] = value[CUT:]


def partial_sums(place, picks, up, down):
    vmem = pl.BlockSpec(memory_space=pltpu.VMEM)
    widths = [cols.stop - cols.start for cols in STREAMS]
    shapes = [jax.ShapeDtypeStruct((rows, w), BF) for w in widths for rows in (CUT, CHUNK - CUT)]
    shapes += [jax.ShapeDtypeStruct((NODES, CHUNK, w), BF) for w in widths]
    return pl.pallas_call(
        partial_kernel,
        out_shape=shapes,
        in_specs=[pl.BlockSpec(memory_space=pltpu.SMEM)] + [vmem] * 3,
        out_specs=[vmem] * len(shapes),
        compiler_params=pltpu.CompilerParams(vmem_limit_bytes=VMEM_LIMIT),
        name="partials",
    )(place, picks, up, down)


def outward_kernel(count, *refs):
    parts, (up, down) = refs[:count], refs[count : count + 2]
    outs, (hold, made) = refs[count + 2 : -2], refs[-2:]
    for i, part in enumerate(parts):
        hold[i] = part[...]

    @pl.loop(0, count)
    def _(i):
        rows = hold[i]
        branch, back = dot_nt(rows[:48], down[...]), dot_nt(rows[32:], up[...])
        made[i, :32, :] = branch[:32].astype(BF)
        line = iota((16, COLS), 0)
        made[i, 32:48, :] = jnp.where(line < 2, branch[32:], back[:16]).astype(BF)
        made[i, 48:, :] = back[16:].astype(BF)

    for i, out in enumerate(outs):
        out[...] = made[i]


def outward(parts, up, down):
    vmem, count = pl.BlockSpec(memory_space=pltpu.VMEM), len(parts)
    return pl.pallas_call(
        functools.partial(outward_kernel, count),
        out_shape=[jax.ShapeDtypeStruct((SENT, COLS), BF)] * count,
        in_specs=[vmem] * (count + 2),
        out_specs=[vmem] * count,
        scratch_shapes=[pltpu.VMEM((count, SENT, FF), BF), pltpu.VMEM((count, SENT, COLS), BF)],
        compiler_params=pltpu.CompilerParams(vmem_limit_bytes=VMEM_LIMIT),
        cost_estimate=pl.CostEstimate(
            flops=4 * count * SENT * COLS * FF, bytes_accessed=4 * COLS * FF, transcendentals=0
        ),
        name="outward",
    )(*parts, up, down)


def settle_kernel(place, meta, *refs):
    parts, outs = refs[:NODES], refs[NODES:]
    r, c = iota((ROWS, SENT), 0), iota((ROWS, SENT), 1)
    line = iota((ROWS, COLS), 0)
    heads = []
    for rows in (((MOST, 0), (MOST + 1, 1), (MOST + 2, 2), (MOST + 3, 3)), ((MOST, 4),)):
        head = jnp.zeros((ROWS, TOK), F32)
        for at, source in rows:
            head = jnp.where(line[:, :TOK] == at, meta[source : source + 1, :], head)
        heads.append(jnp.concatenate([head, jnp.zeros((ROWS, COLS - TOK), F32)], axis=1))
    even = place[2] == 0
    picks = []
    for forward in (even, jnp.logical_not(even)):
        start = jnp.where(forward, 0, 2 * MOST)
        head = jnp.where(forward, heads[0], heads[1])
        for owner in (place[1], 1 - place[1]):
            picks.append((onehot((r < MOST) & (c == r + start + owner * MOST)), head))
    for k, part in enumerate(parts):
        at = lax.rem(place[0] + k, NODES)
        rows = part[...]
        for (select, head), out in zip(picks, outs):
            out[at] = (dot(select, rows) + head).astype(BF)


def settle(place, meta, parts):
    vmem = pl.BlockSpec(memory_space=pltpu.VMEM)
    return pl.pallas_call(
        settle_kernel,
        out_shape=(jax.ShapeDtypeStruct((NODES, ROWS, COLS), BF),) * 4,
        in_specs=[pl.BlockSpec(memory_space=pltpu.SMEM)] + [vmem] * (NODES + 1),
        out_specs=(vmem,) * 4,
        compiler_params=pltpu.CompilerParams(vmem_limit_bytes=VMEM_LIMIT),
        name="settle",
    )(place, meta, *parts)


def patch_kernel(place, fraw, braw, far, far_other, near, near_other, fout, bout):
    first, even = place[1] == 0, place[2] == 0
    near, near_other, far, far_other = near[...], near_other[...], far[...], far_other[...]
    fown, fother = jnp.where(even, far, near), jnp.where(even, far_other, near_other)
    bown, bother = jnp.where(even, near, far), jnp.where(even, near_other, far_other)
    line = iota((ROWS, TOK), 0)
    ones = jnp.ones((ROWS, TOK), BF)
    for raw, own, other, out, scaled in (
        (fraw, fown, fother, fout, True),
        (braw, bown, bother, bout, False),
    ):
        head = own[0, :, :TOK]
        slots = jnp.sum(jnp.where(line == MOST, head.astype(F32), 0.0), axis=0, keepdims=True)
        chosen = onehot((slots == line.astype(F32)) & (line < MOST))
        if scaled:
            three = jnp.where((line > MOST) & (line < MOST + 4), head.astype(F32), 0.0).astype(BF)
            scaling = jnp.concatenate([dot_tn(three, ones)] * (WIDE // TOK), axis=1)
        for j in range(own.shape[0]):
            mine, theirs = own[j], other[j]
            rows = jnp.concatenate(
                [jnp.where(first, mine, theirs), jnp.where(first, theirs, mine)], axis=1
            )
            fresh = dot_tn(chosen, rows)
            if scaled:
                fresh = scaling * fresh
            cols = slice(j * WIDE, (j + 1) * WIDE)
            out[:, cols] = (raw[:, cols].astype(F32) + fresh).astype(BF)


def patch(place, fraw, braw, *rows_sent):
    steps = 4
    strip = pl.BlockSpec((TOK, D // steps), lambda i: (0, i))
    rows = pl.BlockSpec((NODES // steps, ROWS, COLS), lambda i: (i, 0, 0))
    return pl.pallas_call(
        patch_kernel,
        grid=(steps,),
        out_shape=(jax.ShapeDtypeStruct((TOK, D), BF),) * 2,
        in_specs=[pl.BlockSpec(memory_space=pltpu.SMEM), strip, strip] + [rows] * 4,
        out_specs=(strip, strip),
        compiler_params=pltpu.CompilerParams(vmem_limit_bytes=VMEM_LIMIT),
        name="patch",
    )(place, fraw, braw, *rows_sent)


def around(value, steps):
    pairs = [(2 * z + x, 2 * ((z + steps) % NODES) + x) for z in range(NODES) for x in range(2)]
    return lax.ppermute(value, "expert", pairs)


def across_x(value):
    return lax.ppermute(value, "expert", [(e, e ^ 1) for e in range(2 * NODES)])


def section_move(value, target, flip=0):
    sections, experts = lax.axis_size("section"), lax.axis_size("expert")
    pairs = [
        (s * experts + e, target(s) % sections * experts + (e ^ flip))
        for s in range(sections)
        for e in range(experts)
    ]
    return lax.ppermute(value, ("section", "expert"), pairs)


def add(*terms):
    return functools.reduce(lambda a, b: a + b, [t.astype(F32) for t in terms]).astype(BF)


def scatter_ring(right, left, part):
    right, left = around(right, 1), around(left, -1)
    right = jnp.concatenate([add(part[3, :CUT], right), part[3, CUT:]])
    left = jnp.concatenate([part[5, :CUT], add(part[5, CUT:], left)])
    for k in (2, 1):
        right = add(part[k], around(right, 1))
        left = add(part[NODES - k], around(left, -1))
    total = add(part[0], around(right, 1), around(left, -1))
    return total.astype(F32) + across_x(total).astype(F32)


def activate(total):
    before = total[: 2 * MOST]
    hidden = jax.nn.silu(total[2 * MOST : 4 * MOST])
    grad = total[4 * MOST : 6 * MOST]
    sigma = jax.nn.sigmoid(before)
    pre_grad = grad * (sigma * (1.0 + before * (1.0 - sigma)))
    pad = jnp.zeros((SENT - 4 * MOST, total.shape[1]), F32)
    return jnp.concatenate([hidden, pre_grad, pad]).astype(BF)


def gather_ring(mine, up, down):
    half = 32
    back = [None] * NODES
    right, left = around(mine, 1), around(mine, -1)
    made = outward([mine], up, down)
    right, left, back[0] = lax.optimization_barrier((right, left, made[0]))
    for k in (1, 2, 3):
        if k < 3:
            onward = around(right, 1), around(left, -1)
        else:
            onward = around(right[:half], 1), around(left[half:], -1)
        one, two = outward([right, left], up, down)
        back[k], back[NODES - k] = around(one, -k), around(two, k)
        if k > 1:
            onward, one, two, back[k - 1], back[NODES - k + 1] = lax.optimization_barrier(
                (onward, one, two, back[k - 1], back[NODES - k + 1])
            )
        else:
            onward, one, two = lax.optimization_barrier((onward, one, two))
        right, left = onward
    (far,) = outward([jnp.concatenate([right, left])], up, down)
    back[4] = around(far, 4)
    return back


def per_device(
    forward_in,
    backward_saved,
    backward_grad,
    forward_routes,
    forward_gates,
    backward_routes,
    backward_gates,
    up_weight,
    down_weight,
):
    up, down = up_weight[0], down_weight[0].T
    expert = lax.axis_index("expert").astype(jnp.int32)
    section = lax.axis_index("section").astype(jnp.int32)
    place = jnp.stack([expert // 2, expert % 2, section % 2])
    packed, meta = pick(
        forward_routes[0].T,
        forward_gates[0].T,
        backward_routes[0].T,
        backward_gates[0].T,
        forward_in[0],
        backward_saved[0],
        backward_grad[0],
    )
    packed, acts, cot = lax.optimization_barrier((packed, forward_in[0], backward_grad[0]))
    picks = lax.all_to_all(packed, "expert", split_axis=0, concat_axis=0, tiled=True)
    fraw, braw = section_move(acts, lambda s: s + 1), section_move(cot, lambda s: s - 1)
    (right1, left1, right2, left2, part1, part2), fraw, braw = lax.optimization_barrier(
        (partial_sums(place, picks, up, down), fraw, braw)
    )
    totals = [scatter_ring(right1, left1, part1), scatter_ring(right2, left2, part2)]
    mine = jnp.concatenate([activate(total) for total in totals], axis=1)
    back = gather_ring(mine, up, down)
    near, near_other, far, far_other = settle(place, meta, back)
    beside = lambda s: s ^ 1
    beyond = lambda s: s + 1 if s % 2 else s - 1
    far, far_other = section_move(far, beyond), section_move(far_other, beyond, 1)
    near, near_other = section_move(near, beside), section_move(near_other, beside, 1)
    forward_out, backward_out = patch(place, fraw, braw, far, far_other, near, near_other)
    return forward_out[None], backward_out[None]


def solution(mesh):
    row = P("section", "expert", None)
    return jax.shard_map(
        per_device,
        mesh=mesh,
        in_specs=(row, row, row, row, row, row, row, row, P("section", None, "expert")),
        out_specs=(row, row),
        check_vma=False,
    )
```

```python
import functools

import jax
import jax.numpy as jnp
from jax import lax
from jax.experimental import pallas as pl
from jax.experimental.pallas import tpu as pltpu
from jax.sharding import PartitionSpec as P

MOST = 17
TOK = 128
D = 7168
FF = 2432
COLS = 448
NODES = 8
PICK = 56
CHUNK = 104
SENT = 72
ROWS = 24
FIRST = 1280
BF = jnp.bfloat16
F32 = jnp.float32
WIDE = 2 * COLS
VMEM_LIMIT = 24 * 1024 * 1024
VMEM_MOST = 60 * 1024 * 1024
STREAMS = (slice(0, FIRST), slice(FIRST, FF))
CUT = 48


def iota(shape, dim):
    return lax.broadcasted_iota(jnp.int32, shape, dim)


def dot(left, right):
    return jnp.dot(left, right, preferred_element_type=F32)


def dot_tn(left, right):
    return lax.dot_general(left, right, (((0,), (0,)), ((), ())), preferred_element_type=F32)


def dot_nt(left, right):
    return lax.dot_general(left, right, (((1,), (1,)), ((), ())), preferred_element_type=F32)


def onehot(cond):
    return jnp.where(cond, 1.0, 0.0).astype(BF)


def slot_rows(hit):
    wide = jnp.broadcast_to(hit, (TOK, TOK)).astype(BF)
    upto = onehot(iota((TOK, TOK), 0) <= iota((TOK, TOK), 1))
    return jnp.where(wide > 0.5, dot(wide, upto) - 1.0, -1.0)


def placed(slots, start):
    row = iota((PICK, TOK), 0) - start
    return (slots[:PICK] == row.astype(F32)) & (row >= 0)


def pick_kernel(froutes, fgates, broutes, bgates, acts, saved, cot, packed, meta, held, sems):
    sources = (acts, saved, cot)

    strips = 4

    def fetch(j, i):
        cols = pl.ds(pl.multiple_of(j * (D // strips), TOK), D // strips)
        return pltpu.make_async_copy(sources[i].at[:, cols], held.at[i, :, cols], sems.at[j, i])

    for j in range(strips):
        for i in range(3):
            fetch(j, i).start()

    fhits, bhits = froutes[...] == 0, broutes[...] == 0
    fslots = slot_rows(jnp.sum(jnp.where(fhits, 1.0, 0.0), axis=0, keepdims=True))
    bslots = slot_rows(jnp.sum(jnp.where(bhits, 1.0, 0.0), axis=0, keepdims=True))
    fscaling = jnp.sum(jnp.where(fhits, fgates[...], 0.0), axis=0, keepdims=True)
    bscaling = jnp.sum(jnp.where(bhits, bgates[...], 0.0), axis=0, keepdims=True)
    px = onehot(placed(fslots, 0))
    ps = onehot(placed(bslots, MOST))
    ups = placed(bslots, 2 * MOST)
    pu = onehot(ups)
    gate = jnp.sum(jnp.where(ups, bscaling, 0.0), axis=1, keepdims=True)
    hi = fscaling.astype(BF).astype(F32)
    mid = (fscaling - hi).astype(BF).astype(F32)
    low = fscaling - hi - mid
    line = iota((8, TOK), 0)
    rows = jnp.where(line == 0, fslots[:8], bslots[:8])
    for at, value in ((1, hi), (2, mid), (3, low)):
        rows = jnp.where(line == at, value, rows)
    meta[...] = rows

    @pl.loop(0, strips)
    def _(j):
        for i in range(3):
            fetch(j, i).wait()
        for half in range(2):
            k = 2 * j + half
            cols = pl.ds(pl.multiple_of(k * WIDE, TOK), WIDE)
            x, saves, raw = (held[i, :, cols] for i in range(3))
            rows = (dot(px, x) + dot(ps, saves) + gate * dot(pu, raw)).astype(BF)
            packed[2 * k] = rows[:, :COLS]
            packed[2 * k + 1] = rows[:, COLS:]


def pick(froutes, fgates, broutes, bgates, acts, saved, cot):
    vmem = pl.BlockSpec(memory_space=pltpu.VMEM)
    anywhere = pl.BlockSpec(memory_space=pl.ANY)
    return pl.pallas_call(
        pick_kernel,
        in_specs=[vmem] * 4 + [anywhere] * 3,
        out_specs=(vmem,) * 2,
        scratch_shapes=[pltpu.VMEM((3, TOK, D), BF), pltpu.SemaphoreType.DMA((4, 3))],
        out_shape=(
            jax.ShapeDtypeStruct((2 * NODES, PICK, COLS), BF),
            jax.ShapeDtypeStruct((8, TOK), F32),
        ),
        compiler_params=pltpu.CompilerParams(vmem_limit_bytes=VMEM_MOST),
        name="pick",
    )(froutes, fgates, broutes, bgates, acts, saved, cot)


def spread(rows, places):
    r, c = iota((rows, PICK), 0), iota((rows, PICK), 1)
    out = None
    for start, source in places:
        j = r - start
        here = (j >= 0) & (j < MOST) & (c == j + source)
        out = here if out is None else out | here
    return onehot(out)


def partial_kernel(place, picks, up, down, *refs):
    far, sums = refs[:4], refs[4:6]
    tall, low = 72, 40
    edge = 4 * MOST - 64
    inputs, grads = [], []
    for half in range(2):
        for owner in range(2):
            at = half * tall + owner * MOST
            inputs.append(spread(2 * tall + 8, ((at, MOST), (at + 2 * MOST, 0))))
            grads.append(spread(2 * low, ((half * low + edge + owner * MOST, 2 * MOST),)))

    @pl.loop(0, NODES // 2)
    def _(pair):
        blocks = []
        for half in range(2):
            at = 2 * lax.rem(place[0] + 2 * pair + half, NODES)
            blocks += [picks[at], picks[at + 1]]
        rows = sum(dot(e, block) for e, block in zip(inputs, blocks)).astype(BF)
        ends = sum(dot(e, block) for e, block in zip(grads, blocks)).astype(BF)
        for out, cols in zip(sums, STREAMS):
            ups, downs = dot(rows, up[:, cols]), dot(ends, down[:, cols])
            first = iota((16, cols.stop - cols.start), 0) < edge
            for half in range(2):
                k, i, j = 2 * pair + half, half * tall, half * low
                out[k, :64, :] = ups[i : i + 64].astype(BF)
                mixed = jnp.where(first, ups[i + 64 : i + 80], downs[j : j + 16])
                out[k, 64:80, :] = mixed.astype(BF)
                out[k, 80:, :] = downs[j + 16 : j + low].astype(BF)

    for i, out in enumerate(sums):
        value = out[4]
        far[2 * i][...] = value[:CUT]
        far[2 * i + 1][...] = value[CUT:]


def partial_sums(place, picks, up, down):
    vmem = pl.BlockSpec(memory_space=pltpu.VMEM)
    widths = [cols.stop - cols.start for cols in STREAMS]
    shapes = [jax.ShapeDtypeStruct((rows, w), BF) for w in widths for rows in (CUT, CHUNK - CUT)]
    shapes += [jax.ShapeDtypeStruct((NODES, CHUNK, w), BF) for w in widths]
    return pl.pallas_call(
        partial_kernel,
        out_shape=shapes,
        in_specs=[pl.BlockSpec(memory_space=pltpu.SMEM)] + [vmem] * 3,
        out_specs=[vmem] * len(shapes),
        compiler_params=pltpu.CompilerParams(vmem_limit_bytes=VMEM_LIMIT),
        name="partials",
    )(place, picks, up, down)


def outward_kernel(count, *refs):
    parts, (up, down) = refs[:count], refs[count : count + 2]
    outs, (hold, made) = refs[count + 2 : -2], refs[-2:]
    for i, part in enumerate(parts):
        hold[i] = part[...]

    @pl.loop(0, count)
    def _(i):
        rows = hold[i]
        branch, back = dot_nt(rows[:48], down[...]), dot_nt(rows[32:], up[...])
        made[i, :32, :] = branch[:32].astype(BF)
        line = iota((16, COLS), 0)
        made[i, 32:48, :] = jnp.where(line < 2, branch[32:], back[:16]).astype(BF)
        made[i, 48:, :] = back[16:].astype(BF)

    for i, out in enumerate(outs):
        out[...] = made[i]


def outward(parts, up, down):
    vmem, count = pl.BlockSpec(memory_space=pltpu.VMEM), len(parts)
    return pl.pallas_call(
        functools.partial(outward_kernel, count),
        out_shape=[jax.ShapeDtypeStruct((SENT, COLS), BF)] * count,
        in_specs=[vmem] * (count + 2),
        out_specs=[vmem] * count,
        scratch_shapes=[pltpu.VMEM((count, SENT, FF), BF), pltpu.VMEM((count, SENT, COLS), BF)],
        compiler_params=pltpu.CompilerParams(vmem_limit_bytes=VMEM_LIMIT),
        cost_estimate=pl.CostEstimate(
            flops=4 * count * SENT * COLS * FF, bytes_accessed=4 * COLS * FF, transcendentals=0
        ),
        name="outward",
    )(*parts, up, down)


def settle_kernel(place, meta, *refs):
    parts, outs = refs[:NODES], refs[NODES:]
    r, c = iota((ROWS, SENT), 0), iota((ROWS, SENT), 1)
    line = iota((ROWS, COLS), 0)
    heads = []
    for rows in (((MOST, 0), (MOST + 1, 1), (MOST + 2, 2), (MOST + 3, 3)), ((MOST, 4),)):
        head = jnp.zeros((ROWS, TOK), F32)
        for at, source in rows:
            head = jnp.where(line[:, :TOK] == at, meta[source : source + 1, :], head)
        heads.append(jnp.concatenate([head, jnp.zeros((ROWS, COLS - TOK), F32)], axis=1))
    even = place[2] == 0
    picks = []
    for forward in (even, jnp.logical_not(even)):
        start = jnp.where(forward, 0, 2 * MOST)
        head = jnp.where(forward, heads[0], heads[1])
        for owner in (place[1], 1 - place[1]):
            picks.append((onehot((r < MOST) & (c == r + start + owner * MOST)), head))
    for k, part in enumerate(parts):
        at = lax.rem(place[0] + k, NODES)
        rows = part[...]
        for (select, head), out in zip(picks, outs):
            out[at] = (dot(select, rows) + head).astype(BF)


def settle(place, meta, parts):
    vmem = pl.BlockSpec(memory_space=pltpu.VMEM)
    return pl.pallas_call(
        settle_kernel,
        out_shape=(jax.ShapeDtypeStruct((NODES, ROWS, COLS), BF),) * 4,
        in_specs=[pl.BlockSpec(memory_space=pltpu.SMEM)] + [vmem] * (NODES + 1),
        out_specs=(vmem,) * 4,
        compiler_params=pltpu.CompilerParams(vmem_limit_bytes=VMEM_LIMIT),
        name="settle",
    )(place, meta, *parts)


def patch_kernel(place, fraw, braw, far, far_other, near, near_other, fout, bout):
    first, even = place[1] == 0, place[2] == 0
    near, near_other, far, far_other = near[...], near_other[...], far[...], far_other[...]
    fown, fother = jnp.where(even, far, near), jnp.where(even, far_other, near_other)
    bown, bother = jnp.where(even, near, far), jnp.where(even, near_other, far_other)
    line = iota((ROWS, TOK), 0)
    ones = jnp.ones((ROWS, TOK), BF)
    for raw, own, other, out, scaled in (
        (fraw, fown, fother, fout, True),
        (braw, bown, bother, bout, False),
    ):
        head = own[0, :, :TOK]
        slots = jnp.sum(jnp.where(line == MOST, head.astype(F32), 0.0), axis=0, keepdims=True)
        chosen = onehot((slots == line.astype(F32)) & (line < MOST))
        if scaled:
            three = jnp.where((line > MOST) & (line < MOST + 4), head.astype(F32), 0.0).astype(BF)
            scaling = jnp.concatenate([dot_tn(three, ones)] * (WIDE // TOK), axis=1)
        for j in range(own.shape[0]):
            mine, theirs = own[j], other[j]
            rows = jnp.concatenate(
                [jnp.where(first, mine, theirs), jnp.where(first, theirs, mine)], axis=1
            )
            fresh = dot_tn(chosen, rows)
            if scaled:
                fresh = scaling * fresh
            cols = slice(j * WIDE, (j + 1) * WIDE)
            out[:, cols] = (raw[:, cols].astype(F32) + fresh).astype(BF)


def patch(place, fraw, braw, *rows_sent):
    steps = 4
    strip = pl.BlockSpec((TOK, D // steps), lambda i: (0, i))
    rows = pl.BlockSpec((NODES // steps, ROWS, COLS), lambda i: (i, 0, 0))
    return pl.pallas_call(
        patch_kernel,
        grid=(steps,),
        out_shape=(jax.ShapeDtypeStruct((TOK, D), BF),) * 2,
        in_specs=[pl.BlockSpec(memory_space=pltpu.SMEM), strip, strip] + [rows] * 4,
        out_specs=(strip, strip),
        compiler_params=pltpu.CompilerParams(vmem_limit_bytes=VMEM_LIMIT),
        name="patch",
    )(place, fraw, braw, *rows_sent)


def around(value, steps):
    pairs = [(2 * z + x, 2 * ((z + steps) % NODES) + x) for z in range(NODES) for x in range(2)]
    return lax.ppermute(value, "expert", pairs)


def across_x(value):
    return lax.ppermute(value, "expert", [(e, e ^ 1) for e in range(2 * NODES)])


def section_move(value, target, flip=0):
    sections, experts = lax.axis_size("section"), lax.axis_size("expert")
    pairs = [
        (s * experts + e, target(s) % sections * experts + (e ^ flip))
        for s in range(sections)
        for e in range(experts)
    ]
    return lax.ppermute(value, ("section", "expert"), pairs)


def add(*terms):
    return functools.reduce(lambda a, b: a + b, [t.astype(F32) for t in terms]).astype(BF)


def scatter_ring(right, left, part):
    right, left = around(right, 1), around(left, -1)
    right = jnp.concatenate([add(part[3, :CUT], right), part[3, CUT:]])
    left = jnp.concatenate([part[5, :CUT], add(part[5, CUT:], left)])
    for k in (2, 1):
        right = add(part[k], around(right, 1))
        left = add(part[NODES - k], around(left, -1))
    total = add(part[0], around(right, 1), around(left, -1))
    return total.astype(F32) + across_x(total).astype(F32)


def activate(total):
    before = total[: 2 * MOST]
    hidden = jax.nn.silu(total[2 * MOST : 4 * MOST])
    grad = total[4 * MOST : 6 * MOST]
    sigma = jax.nn.sigmoid(before)
    pre_grad = grad * (sigma * (1.0 + before * (1.0 - sigma)))
    pad = jnp.zeros((SENT - 4 * MOST, total.shape[1]), F32)
    return jnp.concatenate([hidden, pre_grad, pad]).astype(BF)


def gather_ring(mine, up, down):
    half = 32
    back = [None] * NODES
    right, left = around(mine, 1), around(mine, -1)
    made = outward([mine], up, down)
    right, left, back[0] = lax.optimization_barrier((right, left, made[0]))
    for k in (1, 2, 3):
        if k < 3:
            onward = around(right, 1), around(left, -1)
        else:
            onward = around(right[:half], 1), around(left[half:], -1)
        one, two = outward([right, left], up, down)
        back[k], back[NODES - k] = around(one, -k), around(two, k)
        if k > 1:
            onward, one, two, back[k - 1], back[NODES - k + 1] = lax.optimization_barrier(
                (onward, one, two, back[k - 1], back[NODES - k + 1])
            )
        else:
            onward, one, two = lax.optimization_barrier((onward, one, two))
        right, left = onward
    (far,) = outward([jnp.concatenate([right, left])], up, down)
    back[4] = around(far, 4)
    return back


def per_device(
    forward_in,
    backward_saved,
    backward_grad,
    forward_routes,
    forward_gates,
    backward_routes,
    backward_gates,
    up_weight,
    down_weight,
):
    up, down = up_weight[0], down_weight[0].T
    expert = lax.axis_index("expert").astype(jnp.int32)
    section = lax.axis_index("section").astype(jnp.int32)
    place = jnp.stack([expert // 2, expert % 2, section % 2])
    packed, meta = pick(
        forward_routes[0].T,
        forward_gates[0].T,
        backward_routes[0].T,
        backward_gates[0].T,
        forward_in[0],
        backward_saved[0],
        backward_grad[0],
    )
    packed, acts, cot = lax.optimization_barrier((packed, forward_in[0], backward_grad[0]))
    picks = lax.all_to_all(packed, "expert", split_axis=0, concat_axis=0, tiled=True)
    fraw, braw = section_move(acts, lambda s: s + 1), section_move(cot, lambda s: s - 1)
    (right1, left1, right2, left2, part1, part2), fraw, braw = lax.optimization_barrier(
        (partial_sums(place, picks, up, down), fraw, braw)
    )
    totals = [scatter_ring(right1, left1, part1), scatter_ring(right2, left2, part2)]
    mine = jnp.concatenate([activate(total) for total in totals], axis=1)
    back = gather_ring(mine, up, down)
    near, near_other, far, far_other = settle(place, meta, back)
    beside = lambda s: s ^ 1
    beyond = lambda s: s + 1 if s % 2 else s - 1
    far, far_other = section_move(far, beyond), section_move(far_other, beyond, 1)
    near, near_other = section_move(near, beside), section_move(near_other, beside, 1)
    forward_out, backward_out = patch(place, fraw, braw, far, far_other, near, near_other)
    return forward_out[None], backward_out[None]


def solution(mesh):
    row = P("section", "expert", None)
    return jax.shard_map(
        per_device,
        mesh=mesh,
        in_specs=(row, row, row, row, row, row, row, row, P("section", None, "expert")),
        out_specs=(row, row),
        check_vma=False,
    )
```
